32 devices in a mesh: grp: 2 (over y), blk: 4 (over x, core), head: 4 (over z).
Axes of the slice: x: 2, y: 2, z: 4, core: 2. Of those that a mesh axis runs over, the one named last changes fastest.
Arguments:
- query_rows: bfloat16 [4096, 8192], P(('grp', 'blk', 'head')), parts along dimension 0, may hold values from -144 to 144
- key_rows: bfloat16 [4096, 1024], P(('grp', 'blk', 'head')), parts along dimension 0, may hold values from -6 to 6
- value_rows: bfloat16 [4096, 1024], P(('grp', 'blk', 'head')), parts along dimension 0, may hold values from -6 to 6
- placement: int32 [8], P('grp'), parts along dimension 0, may hold values from 0 to 3, as said below
- lengths: int32 [4], P('grp'), parts along dimension 0, may hold values from 1 to 512, as said below
Outputs:
- attended: bfloat16 [4096, 8192], P(('grp', 'blk', 'head')), parts along dimension 0
The draws below stay inside these ranges and needn't reach their ends.
There are 2 independent parts, one for each index of `grp`. The reference program is written for one: setup_inputs(seed, part) draws one part's arguments, and reference() takes and returns one part's arrays. A program takes and returns all parts, laid end to end along the dimension named above; each array names one. Nothing has to cross between parts.
Inputs may be any that keep to these rules, and one draw needn't show every extreme that they name: `placement`: a permutation of 0 to 3. `lengths`: exactly one response has the full length 512; the others are shorter.
All inputs are finite; a program needn't handle non-finite values.
Results may differ from the reference program's by a relative error of at most 0.0033.
Values may be sent and summed in bfloat16 or wider, within the bound.
No kernel may reach another device: no remote copies, remote signals or barrier semaphores. Data moves between devices by JAX's collectives and lax.ppermute only.
A program may use at most 64 MiB of HBM per device.

```python
import math
import jax
import jax.numpy as jnp
from jax import lax

QH = 64
KVH = 8
HD = 128
RESP_LEN = 512
BLOCKS = 4
RESPONSES = 2
PROMPT = 1024
TOKENS = 2048


def layout_perm(key):
    return jax.random.permutation(jax.random.fold_in(key, 11), BLOCKS).astype(jnp.int32)


def base_keys(key):
    drawn_rows = jax.random.normal(jax.random.fold_in(key, 21), (TOKENS, KVH * HD), jnp.float32)
    return jnp.clip(drawn_rows, -6.0, 6.0)


def draw_placement(key, part):
    shard_order = layout_perm(key)
    return shard_order


def draw_key_rows(key, part):
    drawn_rows = base_keys(key)
    return drawn_rows.astype(jnp.bfloat16)


def draw_query_rows(key, part):
    key = jax.random.fold_in(key, 5)
    return jnp.clip(2.5 * jax.random.normal(key, (TOKENS, QH * HD), jnp.float32), -15.0, 15.0).astype(jnp.bfloat16)


def draw_lengths(key, part):
    key = jax.random.fold_in(key, 7)
    drawn = jax.random.randint(key, (RESPONSES,), 1, RESP_LEN)
    order = jax.random.permutation(jax.random.fold_in(key, 1), RESPONSES).astype(jnp.int32)
    return jnp.where(order == 0, RESP_LEN, drawn).astype(jnp.int32)


def steps_of(rng, shape, pieces, low, top_value):
    gain = 1.0
    for position, blocks in pieces:
        draws = jax.random.uniform(jax.random.fold_in(jax.random.fold_in(rng, 6), position), (blocks,), jnp.float32, low / len(pieces), top_value / len(pieces))
        gain = gain * jnp.repeat(jnp.exp(draws), shape[position] // blocks).reshape((-1,) + (1,) * (len(shape) - 1 - position))
    return gain


def noise(stream_key, shape, deviation, limit, shards=(), kind=jnp.bfloat16):
    result = jax.random.normal(stream_key, shape, jnp.float32) * deviation
    if len(shards) > 0:
        result = steps_of(stream_key, shape, shards, -0.22, 0.18) * result
    return jnp.clip(result, min=-limit, max=limit).astype(kind)


def setup_inputs(seed: int = 0, part: int = 0) -> dict:
    key_of = jax.random.split(jax.random.key(seed), 6)
    own_keys = jax.random.split(jax.random.fold_in(key_of[5], part), 6)
    query_rows = draw_query_rows(jax.random.fold_in(jax.random.fold_in(key_of[5], part), 71), part)
    key_rows = draw_key_rows(jax.random.fold_in(jax.random.fold_in(key_of[5], part), 71), part)
    value_rows = noise(own_keys[2], (TOKENS, KVH * HD), 1.0, 6.0, ((0, 16),))
    placement = draw_placement(jax.random.fold_in(jax.random.fold_in(key_of[5], part), 71), part)
    lengths = draw_lengths(jax.random.fold_in(jax.random.fold_in(key_of[5], part), 71), part)
    return dict(query_rows=query_rows, key_rows=key_rows, value_rows=value_rows, placement=placement, lengths=lengths)


def reference(query_rows, key_rows, value_rows, placement, lengths):
    score_scale = 1.0 / math.sqrt(HD)
    head_group = QH // KVH
    inverse = jnp.zeros((BLOCKS,), jnp.int32).at[placement].set(jnp.arange(BLOCKS, dtype=jnp.int32))
    query_log = query_rows.reshape(BLOCKS, RESP_LEN, QH, HD)[inverse]
    key_log = key_rows.reshape(BLOCKS, RESP_LEN, KVH, HD)[inverse]
    value_log = value_rows.reshape(BLOCKS, RESP_LEN, KVH, HD)[inverse]
    prompt_keys = key_log[:RESPONSES].reshape(PROMPT, KVH, HD)
    prompt_values = value_log[:RESPONSES].reshape(PROMPT, KVH, HD)
    offsets = jnp.arange(RESP_LEN, dtype=jnp.int32)
    prompt_pos = jnp.arange(PROMPT, dtype=jnp.int32)

    def one_block(items):
        block_id, query_blk, key_blk, value_blk = items
        is_resp = block_id >= RESPONSES
        slot = jnp.clip(block_id - RESPONSES, 0, RESPONSES - 1).astype(jnp.int32)
        resp_len = jnp.where(is_resp, lengths[slot], RESP_LEN)
        query_pos = block_id * RESP_LEN + offsets
        prompt_vis = is_resp | (prompt_pos[None, :] <= query_pos[:, None])
        own_vis = is_resp & (offsets[None, :] <= offsets[:, None]) & (offsets[None, :] < resp_len)
        visible = jnp.concatenate([prompt_vis, own_vis], axis=1)
        keys_all = jnp.concatenate([prompt_keys, key_blk], axis=0).transpose(1, 0, 2)
        values_all = jnp.concatenate([prompt_values, value_blk], axis=0).transpose(1, 0, 2)
        query_grp = query_blk.reshape(RESP_LEN, KVH, head_group, HD).transpose(1, 2, 0, 3)

        def one_kv(parts):
            query_one, key_one, value_one = parts
            scores = jnp.einsum('gqd,sd->gqs', query_one.astype(jnp.float32), key_one.astype(jnp.float32)) * score_scale
            scores = jnp.where(visible[None], scores, -jnp.inf)
            row_max = lax.optimization_barrier(jnp.max(scores, axis=-1))
            weights = jnp.where(visible[None], jnp.exp(scores - row_max[..., None]), 0.0)
            totals = lax.optimization_barrier(jnp.sum(weights, axis=-1))
            rounded = lax.optimization_barrier(weights.astype(jnp.bfloat16)).astype(jnp.float32)
            summed = jnp.einsum('gqs,sd->gqd', rounded, value_one.astype(jnp.float32))
            return summed / totals[..., None]
        outputs = lax.map(one_kv, (query_grp, keys_all, values_all))
        outputs = outputs.transpose(2, 0, 1, 3).reshape(RESP_LEN, QH * HD)
        keep_rows = jnp.logical_not(is_resp) | (offsets < resp_len)
        return (outputs * keep_rows[:, None]).astype(jnp.bfloat16)
    logical = lax.map(one_block, (jnp.arange(BLOCKS, dtype=jnp.int32), query_log, key_log, value_log))
    return logical[placement].reshape(TOKENS, QH * HD)
```

```python
import functools
import math

import jax
import jax.numpy as jnp
from jax import lax
from jax.experimental import pallas as pl
from jax.experimental.pallas import tpu as pltpu
from jax.sharding import PartitionSpec as P

HD = 128
CHUNKS = 2
EXP2_SCALE = math.log2(math.e) / math.sqrt(HD)


def attend_kernel(prompt_count, group, heads_per_tile, info, query, *refs):
    key_refs = refs[: prompt_count + 1]
    value_refs = refs[prompt_count + 1 : 2 * prompt_count + 2]
    out, bias = refs[-2:]
    tokens = query.shape[0]
    block_rows = key_refs[0].shape[0]
    block_id, first_offset, keep_len = info[prompt_count + 1], info[prompt_count + 2], info[prompt_count + 3]

    @pl.when(pl.program_id(0) == 0)
    def _():
        own_offset = first_offset + lax.broadcasted_iota(jnp.int32, (tokens, block_rows), 0)
        key_offset = lax.broadcasted_iota(jnp.int32, (tokens, block_rows), 1)
        bias[...] = jnp.where(key_offset <= own_offset, 0.0, -jnp.inf)

    kept = first_offset + lax.broadcasted_iota(jnp.int32, (tokens, 1), 0) < keep_len
    hidden = [jnp.where(block_id > j, 0.0, jnp.inf).astype(jnp.float32) for j in range(prompt_count)]
    rows = heads_per_tile * tokens
    for tile in range(group // heads_per_tile):
        heads = range(tile * heads_per_tile, (tile + 1) * heads_per_tile)
        query_tile = jnp.concatenate([query[:, h * HD : (h + 1) * HD] for h in heads], axis=0)
        scores = [
            lax.dot_general(query_tile, k[...], (((1,), (1,)), ((), ())), preferred_element_type=jnp.float32)
            for k in key_refs
        ]
        own = scores[prompt_count].reshape(heads_per_tile, tokens, block_rows) + bias[...][None]
        scores[prompt_count] = own.reshape(rows, block_rows)
        row_max = jnp.max(scores[prompt_count], axis=1, keepdims=True)
        for j in range(prompt_count):
            row_max = jnp.maximum(row_max, jnp.max(scores[j], axis=1, keepdims=True) - hidden[j])
        total = jnp.zeros((rows, 1), jnp.float32)
        summed = jnp.zeros((rows, HD), jnp.float32)
        for j in range(prompt_count + 1):
            shift = row_max if j == prompt_count else row_max + hidden[j]
            weights = jnp.exp2((scores[j] - shift) * EXP2_SCALE)
            total += jnp.sum(weights, axis=1, keepdims=True)
            summed += jnp.dot(weights.astype(jnp.bfloat16), value_refs[j][...], preferred_element_type=jnp.float32)
        result = summed / total
        for i, h in enumerate(heads):
            one = jnp.where(kept, result[i * tokens : (i + 1) * tokens], 0.0)
            out[:, h * HD : (h + 1) * HD] = one.astype(out.dtype)


def attend(info, query_rows, kv, chunk, chunks, prompt_count, previous):
    tokens, width = query_rows.shape
    kv_heads = kv.shape[1] // (2 * HD)
    group = width // HD // (kv_heads * chunks)
    block_rows = kv.shape[0] // (2 * prompt_count)

    def kv_spec(place, first):
        return pl.BlockSpec((block_rows, HD), lambda g, info: (info[place], first + g))

    own_spec = pl.BlockSpec((tokens, group * HD), lambda g, info: (0, chunk * kv_heads + g))
    kv_specs = [kv_spec(j, first) for first in (0, kv_heads) for j in range(prompt_count + 1)]
    in_specs, args, aliases = [own_spec, *kv_specs], [info, query_rows] + [kv] * len(kv_specs), {}
    body = functools.partial(attend_kernel, prompt_count, group, 4)
    if previous is not None:
        aliases = {len(args): 0}
        in_specs.append(pl.BlockSpec(memory_space=pl.ANY))
        args.append(previous)
    work = tokens * group * kv_heads * block_rows * (prompt_count + 1)
    return pl.pallas_call(
        body,
        grid_spec=pltpu.PrefetchScalarGridSpec(
            num_scalar_prefetch=1,
            grid=(kv_heads,),
            in_specs=in_specs,
            out_specs=own_spec,
            scratch_shapes=[pltpu.VMEM((tokens, block_rows), jnp.float32)],
        ),
        out_shape=jax.ShapeDtypeStruct(query_rows.shape, query_rows.dtype),
        input_output_aliases=aliases,
        cost_estimate=pl.CostEstimate(flops=4 * work * HD, bytes_accessed=8 << 20, transcendentals=work),
        compiler_params=pltpu.CompilerParams(vmem_limit_bytes=48 << 20),
    )(*args)


def shards(query_rows, key_rows, value_rows, placement, lengths):
    block_count = lax.axis_size("blk")
    prompt_count = block_count // 2
    tokens = query_rows.shape[0]
    my_index = lax.axis_index("blk")
    block_id = placement[my_index]
    slot = jnp.clip(block_id - prompt_count, 0, prompt_count - 1)
    block_rows = tokens * lax.axis_size("head")
    keep_len = jnp.where(block_id >= prompt_count, lengths[slot], block_rows)
    inverse = jnp.sum(
        jnp.where(placement[None, :] == jnp.arange(prompt_count)[:, None], jnp.arange(block_count)[None, :], 0), axis=1
    )
    first_offset = lax.axis_index("head") * tokens
    info = jnp.concatenate([inverse, jnp.stack([my_index, block_id, first_offset, keep_len])]).astype(jnp.int32)

    width = key_rows.shape[1] // CHUNKS
    gathered = []
    for c in range(CHUNKS):
        columns = slice(c * width, (c + 1) * width)
        packed = jnp.concatenate([key_rows[:, columns], value_rows[:, columns]], axis=1)
        gathered.append(lax.all_gather(packed, ("blk", "head"), axis=0, tiled=True))
    out = None
    for c in range(CHUNKS):
        out = attend(info, query_rows, gathered[c], c, CHUNKS, prompt_count, out)
    return out


def solution(mesh):
    rows = P(("grp", "blk", "head"), None)
    return jax.shard_map(
        shards,
        mesh=mesh,
        in_specs=(rows, rows, rows, P("grp"), P("grp")),
        out_specs=rows,
        check_vma=False,
    )
```

```python
import functools
import math

import jax
import jax.numpy as jnp
from jax import lax
from jax.experimental import pallas as pl
from jax.experimental.pallas import tpu as pltpu
from jax.sharding import PartitionSpec as P

HD = 128
CHUNKS = 2
CORES = 2
EXP2_SCALE = math.log2(math.e) / math.sqrt(HD)


def attend_kernel(sizes, info, query, *refs):
    prompt_count, chips, ring, group, heads_per_tile = sizes
    slots = prompt_count + 1
    pieces, (out, held, bias, sems) = refs[: chips * CORES * ring], refs[-4:]
    tokens = query.shape[0]
    block_rows = ring * tokens
    width = held.shape[2] // 2
    block_id, first_offset, keep_len = info[0], info[1], info[2]
    kv_head = pl.program_id(0)

    def place(piece, slot, hop):
        row = pl.multiple_of(info[3 + slots + hop], tokens)
        return pltpu.make_async_copy(piece, held.at[slot, pl.ds(row, tokens)], sems.at[slot, hop])

    @pl.when(kv_head == 0)
    def _():
        for slot in range(slots):
            for source in range(chips * CORES):

                @pl.when(info[3 + slot] == source)
                def _():
                    for hop in range(ring):
                        place(pieces[source * ring + hop], slot, hop).start()

        own_offset = first_offset + lax.broadcasted_iota(jnp.int32, (tokens, block_rows), 0)
        key_offset = lax.broadcasted_iota(jnp.int32, (tokens, block_rows), 1)
        bias[...] = jnp.where(key_offset <= own_offset, 0.0, -jnp.inf)
        for slot in range(slots):
            for hop in range(ring):
                place(pieces[0], slot, hop).wait()

    kept = first_offset + lax.broadcasted_iota(jnp.int32, (tokens, 1), 0) < keep_len
    hidden = [jnp.where(block_id > j, 0.0, jnp.inf).astype(jnp.float32) for j in range(prompt_count)]
    rows = heads_per_tile * tokens
    column = pl.multiple_of(kv_head * HD, HD)
    keys = [held[j, :, pl.ds(column, HD)] for j in range(slots)]
    values = [held[j, :, pl.ds(pl.multiple_of(width + column, HD), HD)] for j in range(slots)]
    for tile in range(group // heads_per_tile):
        heads = range(tile * heads_per_tile, (tile + 1) * heads_per_tile)
        query_tile = jnp.concatenate([query[:, h * HD : (h + 1) * HD] for h in heads], axis=0)
        scores = [
            lax.dot_general(query_tile, k, (((1,), (1,)), ((), ())), preferred_element_type=jnp.float32) for k in keys
        ]
        own = scores[prompt_count].reshape(heads_per_tile, tokens, block_rows) + bias[...][None]
        scores[prompt_count] = own.reshape(rows, block_rows)
        row_max = jnp.max(scores[prompt_count], axis=1, keepdims=True)
        for j in range(prompt_count):
            row_max = jnp.maximum(row_max, jnp.max(scores[j], axis=1, keepdims=True) - hidden[j])
        total = jnp.zeros((rows, 1), jnp.float32)
        summed = jnp.zeros((rows, HD), jnp.float32)
        for j in range(slots):
            shift = row_max if j == prompt_count else row_max + hidden[j]
            weights = jnp.exp2((scores[j] - shift) * EXP2_SCALE)
            total += jnp.sum(weights, axis=1, keepdims=True)
            summed += jnp.dot(weights.astype(jnp.bfloat16), values[j], preferred_element_type=jnp.float32)
        result = summed / total
        for i, h in enumerate(heads):
            one = jnp.where(kept, result[i * tokens : (i + 1) * tokens], 0.0)
            out[:, h * HD : (h + 1) * HD] = one.astype(out.dtype)


def attend(info, query_rows, pieces, chunk, sizes, previous):
    prompt_count, chips, ring, group, _ = sizes
    tokens, width = query_rows.shape
    piece_width = pieces[0].shape[1]
    kv_heads = piece_width // (2 * HD)
    slots = prompt_count + 1
    own_spec = pl.BlockSpec((tokens, group * HD), lambda g, info: (0, chunk * kv_heads + g))
    whole = pl.BlockSpec(memory_space=pl.ANY)
    in_specs, args, aliases = [own_spec] + [whole] * len(pieces), [info, query_rows, *pieces], {}
    if previous is not None:
        aliases = {len(args): 0}
        in_specs.append(whole)
        args.append(previous)
    work = tokens * group * kv_heads * ring * tokens * slots
    return pl.pallas_call(
        functools.partial(attend_kernel, sizes),
        grid_spec=pltpu.PrefetchScalarGridSpec(
            num_scalar_prefetch=1,
            grid=(kv_heads,),
            in_specs=in_specs,
            out_specs=own_spec,
            scratch_shapes=[
                pltpu.VMEM((slots, ring * tokens, piece_width), jnp.bfloat16),
                pltpu.VMEM((tokens, ring * tokens), jnp.float32),
                pltpu.SemaphoreType.DMA((slots, ring)),
            ],
        ),
        out_shape=jax.ShapeDtypeStruct(query_rows.shape, query_rows.dtype),
        input_output_aliases=aliases,
        cost_estimate=pl.CostEstimate(flops=4 * work * HD, bytes_accessed=8 << 20, transcendentals=work),
        compiler_params=pltpu.CompilerParams(vmem_limit_bytes=48 << 20),
    )(*args)


def gather_pieces(own, chips):
    ring, blocks = lax.axis_size("head"), chips * CORES
    column = [own]
    for _ in range(ring - 1):
        column.append(lax.ppermute(column[-1], "head", [(i, (i + 1) % ring) for i in range(ring)]))
    planes = [column]
    for _ in range(chips - 1):
        planes.append(
            [lax.ppermute(x, "blk", [(i, (i + CORES) % blocks) for i in range(blocks)]) for x in planes[-1]]
        )
    pieces = []
    for plane in planes:
        pieces += plane
        pieces += [lax.ppermute(x, "blk", [(i, i ^ 1) for i in range(blocks)]) for x in plane]
    return pieces


def shards(query_rows, key_rows, value_rows, placement, lengths):
    block_count = lax.axis_size("blk")
    ring = lax.axis_size("head")
    prompt_count = block_count // 2
    chips = block_count // CORES
    tokens = query_rows.shape[0]
    my_index = lax.axis_index("blk")
    my_head = lax.axis_index("head")
    block_id = placement[my_index]
    slot = jnp.clip(block_id - prompt_count, 0, prompt_count - 1)
    keep_len = jnp.where(block_id >= prompt_count, lengths[slot], ring * tokens)
    inverse = jnp.sum(
        jnp.where(placement[None, :] == jnp.arange(prompt_count)[:, None], jnp.arange(block_count)[None, :], 0), axis=1
    )
    chips_back = (my_index // CORES - inverse // CORES) % chips
    source = chips_back * CORES + (my_index + inverse) % CORES
    rows = (my_head - jnp.arange(ring)) % ring * tokens
    fixed = jnp.stack([block_id, my_head * tokens, keep_len])
    info = jnp.concatenate([fixed, source, jnp.zeros((1,), jnp.int32), rows]).astype(jnp.int32)

    group = query_rows.shape[1] // key_rows.shape[1]
    sizes = (prompt_count, chips, ring, group, 4)
    width = key_rows.shape[1] // CHUNKS
    pieces = []
    for c in range(CHUNKS):
        columns = slice(c * width, (c + 1) * width)
        packed = jnp.concatenate([key_rows[:, columns], value_rows[:, columns]], axis=1)
        pieces.append(gather_pieces(packed, chips))
    out = None
    for c in range(CHUNKS):
        out = attend(info, query_rows, pieces[c], c, sizes, out)
    return out


def solution(mesh):
    rows = P(("grp", "blk", "head"), None)
    return jax.shard_map(
        shards,
        mesh=mesh,
        in_specs=(rows, rows, rows, P("grp"), P("grp")),
        out_specs=rows,
        check_vma=False,
    )
```

```python
import functools
import math

import jax
import jax.numpy as jnp
from jax import lax
from jax.experimental import pallas as pl
from jax.experimental.pallas import tpu as pltpu
from jax.sharding import PartitionSpec as P

HD = 128
CORES = 2
HEADS_PER_TILE = 2
EXP2_SCALE = math.log2(math.e) / math.sqrt(HD)
LEAST_TOTAL, MOST_TOTAL = 1e-20, 1e30


def matmul_nt(a, b):
    return lax.dot_general(a, b, (((1,), (1,)), ((), ())), preferred_element_type=jnp.float32)


class Place:
    def __init__(self, sizes, placement, lengths):
        self.prompt_count, self.chips, self.ring, self.tokens = sizes
        self.blocks = self.chips * CORES
        self.index, self.head = lax.axis_index("blk"), lax.axis_index("head")
        self.placement = placement
        self.block = placement[self.index]
        slot = jnp.clip(self.block - self.prompt_count, 0, self.prompt_count - 1)
        rows = self.ring * self.tokens
        self.keep = jnp.where(self.block >= self.prompt_count, lengths[slot], rows)

    def source(self, slot):
        found = jnp.int32(0)
        for b in range(self.blocks):
            found = jnp.where(self.placement[b] == slot, b, found)
        found = jnp.where(slot == self.prompt_count, self.index, found)
        chips_back = lax.rem(self.index // CORES - found // CORES + self.chips, self.chips)
        return chips_back * CORES + lax.rem(self.index + found, CORES)

    def visible(self, slot, hop):
        return jnp.where(slot == self.prompt_count, self.head >= hop, self.block > slot)

    def kept(self):
        offsets = self.head * self.tokens + lax.broadcasted_iota(jnp.int32, (self.tokens, 1), 0)
        return offsets < self.keep


def exact(here, pieces, query, out, held, sem, kv_head, kv_heads, group):
    slots, tokens, ring = here.prompt_count + 1, here.tokens, here.ring
    rows = ring * tokens

    def fetch(slot, carry):
        wanted = here.source(slot)
        for source in range(here.blocks):

            @pl.when(wanted == source)
            def _():
                for hop in range(ring):
                    first = pl.multiple_of(lax.rem(here.head - hop + ring, ring) * tokens, tokens)
                    for i in range(2):
                        column = pl.multiple_of((i * kv_heads + kv_head) * HD, HD)
                        copy = pltpu.make_async_copy(
                            pieces[source * ring + hop].at[:, pl.ds(column, HD)],
                            held.at[slot, pl.ds(first, tokens), pl.ds(i * HD, HD)],
                            sem,
                        )
                        copy.start()
                        copy.wait()

        return carry

    lax.fori_loop(0, slots, fetch, 0)
    own_offset = here.head * tokens + lax.broadcasted_iota(jnp.int32, (tokens, rows), 0)
    key_offset = lax.broadcasted_iota(jnp.int32, (tokens, rows), 1)

    def one_head(head, carry):
        columns = pl.ds(pl.multiple_of(head * HD, HD), HD)
        query_one = query[:, columns]

        def score(slot):
            prompt_end = jnp.where(here.block > slot, rows, -1)
            newest = jnp.where(slot == here.prompt_count, own_offset, prompt_end)
            return jnp.where(key_offset <= newest, matmul_nt(query_one, held[slot, :, :HD]), -jnp.inf)

        row_max = lax.fori_loop(
            0,
            slots,
            lambda j, best: jnp.maximum(best, jnp.max(score(j), axis=1, keepdims=True)),
            jnp.full((tokens, 1), -jnp.inf, jnp.float32),
        )

        def add(slot, carry):
            total, summed = carry
            weights = jnp.exp2((score(slot) - row_max) * EXP2_SCALE)
            total += jnp.sum(weights, axis=1, keepdims=True)
            value = held[slot, :, HD:]
            return total, summed + jnp.dot(weights.astype(jnp.bfloat16), value, preferred_element_type=jnp.float32)

        zeros = jnp.zeros((tokens, 1), jnp.float32), jnp.zeros((tokens, HD), jnp.float32)
        total, summed = lax.fori_loop(0, slots, add, zeros)
        out[:, columns] = jnp.where(here.kept(), summed / total, 0.0).astype(out.dtype)
        return carry

    lax.fori_loop(0, group, one_head, 0)


def fold_kernel(sizes, hops, first, last, placement, lengths, query, *refs):
    prompt_count, chips, ring, tokens = sizes
    slots = prompt_count + 1
    here = Place(sizes, placement, lengths)
    used = list(range(ring)) if last else list(hops)
    refs = list(refs)
    pieces = [refs.pop(0) for _ in range(here.blocks * len(used))]
    before = None if first else refs.pop(0)
    out, held, ones, bias, sems = refs[:5]
    kv_head, kv_heads = pl.program_id(0), pl.num_programs(0)
    group = query.shape[1] // HD
    width = held.shape[1] // 2
    order = list(reversed(hops))
    masked = bias.shape[1]

    @pl.when(kv_head == 0)
    def _():
        def at(slot, i):
            return pl.ds(pl.multiple_of((slot * len(order) + i) * tokens, tokens), tokens)

        def fetch(slot, carry):
            wanted = here.source(slot)
            for source in range(here.blocks):

                @pl.when(wanted == source)
                def _():
                    for i, hop in enumerate(order):
                        piece = pieces[source * len(used) + used.index(hop)]
                        pltpu.make_async_copy(piece, held.at[at(slot, i)], sems.at[slot, i]).start()

            return carry

        def finish(slot, carry):
            for i, hop in enumerate(order):
                pltpu.make_async_copy(pieces[0], held.at[at(slot, i)], sems.at[slot, i]).wait()
                seen = here.visible(slot, hop)
                ones[at(slot, i)] = jnp.full((tokens, HD), jnp.where(seen, 1.0, 0.0), jnp.float32).astype(jnp.bfloat16)

                @pl.when(jnp.logical_not(seen))
                def _():
                    held[at(slot, i)] = jnp.zeros((tokens, held.shape[1]), held.dtype)

            return carry

        lax.fori_loop(0, slots, fetch, 0)
        if first:
            own = lax.broadcasted_iota(jnp.int32, (tokens, masked), 0)
            key = lax.broadcasted_iota(jnp.int32, (tokens, masked), 1) - (masked - tokens)
            bias[...] = jnp.where(key <= own, 0.0, -jnp.inf)
        lax.fori_loop(0, slots, finish, 0)

    key = held[:, pl.ds(pl.multiple_of(kv_head * HD, HD), HD)]
    value = held[:, pl.ds(pl.multiple_of(width + kv_head * HD, HD), HD)]
    value = jnp.concatenate([value, ones[...]], axis=1)
    kept = here.kept()
    least = jnp.full((tokens, HD), jnp.inf, jnp.float32)
    most = jnp.zeros((tokens, HD), jnp.float32)
    for tile in range(group // HEADS_PER_TILE):
        heads = range(tile * HEADS_PER_TILE, (tile + 1) * HEADS_PER_TILE)
        query_tile = jnp.concatenate([query[:, h * HD : (h + 1) * HD] for h in heads], axis=0)
        scores = matmul_nt(query_tile, key) * EXP2_SCALE
        if first:
            split = scores.shape[1] - masked
            tail = scores[:, split:].reshape(HEADS_PER_TILE, tokens, masked) + bias[...][None]
            tail = tail.reshape(HEADS_PER_TILE * tokens, masked)
            scores = tail if split == 0 else jnp.concatenate([scores[:, :split], tail], axis=1)
        weights = jnp.exp2(scores).astype(jnp.bfloat16)
        summed = jnp.dot(weights, value, preferred_element_type=jnp.float32)
        for i, h in enumerate(heads):
            columns = slice(h * 2 * HD, (h + 1) * 2 * HD)
            part = summed[i * tokens : (i + 1) * tokens]
            if not first:
                part = part + before[:, columns]
            if last:
                total = part[:, HD:]
                least, most = jnp.minimum(least, total), jnp.maximum(most, total)
                out[:, h * HD : (h + 1) * HD] = jnp.where(kept, part[:, :HD] / total, 0.0).astype(out.dtype)
            else:
                out[:, columns] = part
    if last:
        safe = (jnp.min(least) > LEAST_TOTAL) & (jnp.max(most) < MOST_TOTAL)

        @pl.when(jnp.logical_not(safe))
        def _():
            exact(here, pieces, query, out, refs[5], refs[6], kv_head, kv_heads, group)


def fold(placement, lengths, query_rows, pieces, sizes, hops, before, last):
    prompt_count, chips, ring, tokens = sizes
    slots, blocks = prompt_count + 1, chips * CORES
    first = before is None
    width = query_rows.shape[1]
    kv_width = pieces[0][0].shape[1] // 2
    kv_heads = kv_width // HD
    group = width // kv_width
    whole = pl.BlockSpec(memory_space=pl.ANY)

    def per_head(columns):
        return pl.BlockSpec((tokens, columns), lambda g, *_: (0, g))

    used = range(ring) if last else hops
    operands = [pieces[source][hop] for source in range(blocks) for hop in used]
    in_specs, args = [per_head(group * HD)] + [whole] * len(operands), [query_rows, *operands]
    if not first:
        in_specs.append(per_head(group * 2 * HD))
        args.append(before)
    keys = slots * len(hops) * tokens
    masked = tokens if tokens % HD == 0 else keys
    scratch = [
        pltpu.VMEM((keys, 2 * kv_width), jnp.bfloat16),
        pltpu.VMEM((keys, HD), jnp.bfloat16),
        pltpu.VMEM((tokens, masked), jnp.float32),
        pltpu.SemaphoreType.DMA((slots, len(hops))),
    ]
    if last:
        scratch += [pltpu.VMEM((slots, ring * tokens, 2 * HD), jnp.bfloat16), pltpu.SemaphoreType.DMA]
        out_shape, out_spec = jax.ShapeDtypeStruct((tokens, width), query_rows.dtype), per_head(group * HD)
    else:
        out_shape, out_spec = jax.ShapeDtypeStruct((tokens, 2 * width), jnp.float32), per_head(group * 2 * HD)
    work = tokens * group * kv_heads * keys
    return pl.pallas_call(
        functools.partial(fold_kernel, sizes, hops, first, last),
        grid_spec=pltpu.PrefetchScalarGridSpec(
            num_scalar_prefetch=2, grid=(kv_heads,), in_specs=in_specs, out_specs=out_spec, scratch_shapes=scratch
        ),
        out_shape=out_shape,
        cost_estimate=pl.CostEstimate(flops=6 * work * HD, bytes_accessed=12 << 20, transcendentals=work),
        compiler_params=pltpu.CompilerParams(vmem_limit_bytes=40 << 20),
    )(placement, lengths, *args)


def gather_pieces(own, chips):
    ring, blocks = lax.axis_size("head"), chips * CORES
    column = [own]
    for _ in range(ring - 1):
        column.append(lax.ppermute(column[-1], "head", [(i, (i + 1) % ring) for i in range(ring)]))
    planes = [column]
    for _ in range(chips - 1):
        planes.append(
            [lax.ppermute(x, "blk", [(i, (i + CORES) % blocks) for i in range(blocks)]) for x in planes[-1]]
        )
    pieces = []
    for plane in planes:
        pieces.append(plane)
        pieces.append([lax.ppermute(x, "blk", [(i, i ^ 1) for i in range(blocks)]) for x in plane])
    return pieces


def shards(query_rows, key_rows, value_rows, placement, lengths):
    block_count, ring = lax.axis_size("blk"), lax.axis_size("head")
    sizes = (block_count // 2, block_count // CORES, ring, query_rows.shape[0])
    pieces = gather_pieces(jnp.concatenate([key_rows, value_rows], axis=1), sizes[1])
    state = None
    for hops in (tuple(range(ring - 2)), (ring - 2,), (ring - 1,)):
        state = fold(placement, lengths, query_rows, pieces, sizes, hops, state, hops[-1] == ring - 1)
    return state


def solution(mesh):
    rows = P(("grp", "blk", "head"), None)
    return jax.shard_map(
        shards,
        mesh=mesh,
        in_specs=(rows, rows, rows, P("grp"), P("grp")),
        out_specs=rows,
        check_vma=False,
    )
```

```python
import functools
import math

import jax
import jax.numpy as jnp
from jax import lax
from jax.experimental import pallas as pl
from jax.experimental.pallas import tpu as pltpu
from jax.sharding import PartitionSpec as P

HD = 128
CORES = 2
HEADS_PER_TILE = 2
SPLIT = (5, 8)
EXP2_SCALE = math.log2(math.e) / math.sqrt(HD)
LEAST_TOTAL, MOST_TOTAL = 1e-20, 1e30


def matmul_nt(a, b):
    return lax.dot_general(a, b, (((1,), (1,)), ((), ())), preferred_element_type=jnp.float32)


class Place:
    def __init__(self, sizes, placement, lengths):
        self.prompt_count, self.chips, self.ring, self.tokens = sizes
        self.blocks = self.chips * CORES
        self.index, self.head = lax.axis_index("blk"), lax.axis_index("head")
        self.placement = placement
        self.block = placement[self.index]
        slot = jnp.clip(self.block - self.prompt_count, 0, self.prompt_count - 1)
        rows = self.ring * self.tokens
        self.keep = jnp.where(self.block >= self.prompt_count, lengths[slot], rows)

    def source(self, slot):
        found = jnp.int32(0)
        for b in range(self.blocks):
            found = jnp.where(self.placement[b] == slot, b, found)
        found = jnp.where(slot == self.prompt_count, self.index, found)
        chips_back = lax.rem(self.index // CORES - found // CORES + self.chips, self.chips)
        return chips_back * CORES + lax.rem(self.index + found, CORES)

    def first_key(self, slot):
        own = (self.ring - 1 - self.head) * self.tokens
        return jnp.where(slot == self.prompt_count, own, jnp.where(self.block > slot, 0, self.ring * self.tokens))

    def kept(self):
        offsets = self.head * self.tokens + lax.broadcasted_iota(jnp.int32, (self.tokens, 1), 0)
        return offsets < self.keep


def exact(here, query, key, value, out, group):
    slots, tokens, rows = here.prompt_count + 1, here.tokens, here.ring * here.tokens
    key_row = lax.broadcasted_iota(jnp.int32, (tokens, rows), 1)
    newest_own = rows - tokens + lax.broadcasted_iota(jnp.int32, (tokens, rows), 0)

    def one_head(head, carry):
        columns = pl.ds(pl.multiple_of(head * HD, HD), HD)
        query_one = query[:, columns]

        def part(ref, slot):
            return ref[pl.ds(pl.multiple_of(slot * rows, rows), rows), :]

        def score(slot):
            newest = jnp.where(slot == here.prompt_count, newest_own, rows)
            seen = (key_row >= here.first_key(slot)) & (key_row <= newest)
            return jnp.where(seen, matmul_nt(query_one, part(key, slot)), -jnp.inf)

        row_max = lax.fori_loop(
            0,
            slots,
            lambda j, best: jnp.maximum(best, jnp.max(score(j), axis=1, keepdims=True)),
            jnp.full((tokens, 1), -jnp.inf, jnp.float32),
        )

        def add(slot, carry):
            total, summed = carry
            weights = jnp.exp2((score(slot) - row_max) * EXP2_SCALE)
            total += jnp.sum(weights, axis=1, keepdims=True)
            weights = weights.astype(jnp.bfloat16)
            return total, summed + jnp.dot(weights, part(value, slot), preferred_element_type=jnp.float32)

        zeros = jnp.zeros((tokens, 1), jnp.float32), jnp.zeros((tokens, HD), jnp.float32)
        total, summed = lax.fori_loop(0, slots, add, zeros)
        out[:, columns] = jnp.where(here.kept(), summed / total, 0.0).astype(out.dtype)
        return carry

    lax.fori_loop(0, group, one_head, 0)


def attend_kernel(sizes, placement, lengths, query, *refs):
    prompt_count, chips, ring, tokens = sizes
    slots = prompt_count + 1
    here = Place(sizes, placement, lengths)
    pieces, (out, held, ones, bias, sems) = refs[: here.blocks * ring], refs[-5:]
    kv_head, width = pl.program_id(0), held.shape[1] // 2
    group = query.shape[1] // HD
    masked = bias.shape[1]

    @pl.when(kv_head == 0)
    def _():
        def at(slot, hop):
            return pl.ds(pl.multiple_of((slot * ring + ring - 1 - hop) * tokens, tokens), tokens)

        def fetch(slot, carry):
            wanted = here.source(slot)
            for source in range(here.blocks):

                @pl.when(wanted == source)
                def _():
                    for hop in range(ring):
                        piece = pieces[source * ring + hop]
                        pltpu.make_async_copy(piece, held.at[at(slot, hop)], sems.at[slot, hop]).start()

            return carry

        def finish(slot, carry):
            for hop in range(ring):
                pltpu.make_async_copy(pieces[0], held.at[at(slot, hop)], sems.at[slot, hop]).wait()
                seen = (ring - 1 - hop) * tokens >= here.first_key(slot)
                ones[at(slot, hop)] = jnp.full((tokens, HD), jnp.where(seen, 1.0, 0.0), jnp.float32).astype(ones.dtype)

                @pl.when(jnp.logical_not(seen))
                def _():
                    held[at(slot, hop)] = jnp.zeros((tokens, held.shape[1]), held.dtype)

            return carry

        lax.fori_loop(0, slots, fetch, 0)
        own = lax.broadcasted_iota(jnp.int32, (tokens, masked), 0)
        key = lax.broadcasted_iota(jnp.int32, (tokens, masked), 1) - (masked - tokens)
        bias[...] = jnp.where(key <= own, 0.0, -jnp.inf)
        lax.fori_loop(0, slots, finish, 0)

    key = held.at[:, pl.ds(pl.multiple_of(kv_head * HD, HD), HD)]
    value = held.at[:, pl.ds(pl.multiple_of(width + kv_head * HD, HD), HD)]
    keys, values = key[...], jnp.concatenate([value[...], ones[...]], axis=1)
    kept = here.kept()
    least = jnp.full((tokens, HD), jnp.inf, jnp.float32)
    most = jnp.zeros((tokens, HD), jnp.float32)
    for tile in range(group // HEADS_PER_TILE):
        heads = range(tile * HEADS_PER_TILE, (tile + 1) * HEADS_PER_TILE)
        query_tile = jnp.concatenate([query[:, h * HD : (h + 1) * HD] for h in heads], axis=0)
        scores = matmul_nt(query_tile, keys) * EXP2_SCALE
        split = scores.shape[1] - masked
        tail = scores[:, split:].reshape(HEADS_PER_TILE, tokens, masked) + bias[...][None]
        tail = tail.reshape(HEADS_PER_TILE * tokens, masked)
        scores = tail if split == 0 else jnp.concatenate([scores[:, :split], tail], axis=1)
        weights = jnp.exp2(scores).astype(jnp.bfloat16)
        summed = jnp.dot(weights, values, preferred_element_type=jnp.float32)
        for i, h in enumerate(heads):
            part = summed[i * tokens : (i + 1) * tokens]
            total = part[:, HD:]
            least, most = jnp.minimum(least, total), jnp.maximum(most, total)
            out[:, h * HD : (h + 1) * HD] = jnp.where(kept, part[:, :HD] / total, 0.0).astype(out.dtype)
    safe = (jnp.min(least) > LEAST_TOTAL) & (jnp.max(most) < MOST_TOTAL)

    @pl.when(jnp.logical_not(safe))
    def _():
        exact(here, query, key, value, out, group)


def attend(placement, lengths, query_rows, pieces, sizes, kv_heads, first_head, previous):
    prompt_count, chips, ring, tokens = sizes
    slots = prompt_count + 1
    piece_width = pieces[0].shape[1]
    group = query_rows.shape[1] // HD // kv_heads
    chunk_heads = piece_width // (2 * HD)
    own_spec = pl.BlockSpec((tokens, group * HD), lambda g, *_: (0, first_head + g))
    whole = pl.BlockSpec(memory_space=pl.ANY)
    in_specs, args, aliases = [own_spec] + [whole] * len(pieces), [placement, lengths, query_rows, *pieces], {}
    if previous is not None:
        aliases = {len(args): 0}
        in_specs.append(whole)
        args.append(previous)
    keys = slots * ring * tokens
    masked = tokens if tokens % HD == 0 else keys
    work = tokens * group * chunk_heads * keys
    return pl.pallas_call(
        functools.partial(attend_kernel, sizes),
        grid_spec=pltpu.PrefetchScalarGridSpec(
            num_scalar_prefetch=2,
            grid=(chunk_heads,),
            in_specs=in_specs,
            out_specs=own_spec,
            scratch_shapes=[
                pltpu.VMEM((keys, piece_width), jnp.bfloat16),
                pltpu.VMEM((keys, HD), jnp.bfloat16),
                pltpu.VMEM((tokens, masked), jnp.float32),
                pltpu.SemaphoreType.DMA((slots, ring)),
            ],
        ),
        out_shape=jax.ShapeDtypeStruct(query_rows.shape, query_rows.dtype),
        input_output_aliases=aliases,
        cost_estimate=pl.CostEstimate(flops=6 * work * HD, bytes_accessed=8 << 20, transcendentals=work),
        compiler_params=pltpu.CompilerParams(vmem_limit_bytes=40 << 20),
    )(*args)


def after(x, *others):
    return lax.optimization_barrier((x, *others))[0]


def shards(query_rows, key_rows, value_rows, placement, lengths):
    blocks, ring = lax.axis_size("blk"), lax.axis_size("head")
    chips = blocks // CORES
    sizes = (blocks // 2, chips, ring, query_rows.shape[0])
    kv_heads = key_rows.shape[1] // HD
    cut = kv_heads * SPLIT[0] // SPLIT[1]

    def next_hop(x):
        return lax.ppermute(x, "head", [(i, (i + 1) % ring) for i in range(ring)])

    def next_chip(x):
        return lax.ppermute(x, "blk", [(i, (i + CORES) % blocks) for i in range(blocks)])

    def other_core(x):
        return lax.ppermute(x, "blk", [(i, i ^ 1) for i in range(blocks)])

    def packed(columns):
        return jnp.concatenate([key_rows[:, columns], value_rows[:, columns]], axis=1)

    def collect(planes, last_after):
        for _ in range(chips - len(planes)):
            planes.append([next_chip(x) for x in planes[-1]])
        if last_after is not None:
            planes[-1][-1] = after(planes[-1][-1], last_after)
        pieces = []
        for plane in planes:
            pieces += plane
            pieces += [other_core(x) for x in plane]
        return pieces

    own_a, own_b = packed(slice(0, cut * HD)), packed(slice(cut * HD, kv_heads * HD))
    column_a, across_a = [own_a], [next_chip(own_a)]
    column_b, across_b = [own_b], [next_chip(own_b)]
    for hop in range(1, ring):
        waits = ([across_a[hop - 2]] if hop > 1 else []) + ([across_b[0]] if hop == 3 else [])
        column_a.append(next_hop(after(column_a[-1], *waits) if waits else column_a[-1]))
        across_a.append(next_chip(column_a[-1]))
    for hop in range(1, ring):
        column_b.append(next_hop(after(column_b[-1], column_a[-2] if hop == 1 else column_a[-1], across_a[hop - 3 + ring - 2])))
        across_b.append(next_chip(column_b[-1]))
    out = attend(placement, lengths, query_rows, collect([column_a, across_a], None), sizes, kv_heads, 0, None)
    pieces_b = collect([column_b, across_b], out)
    return attend(placement, lengths, query_rows, pieces_b, sizes, kv_heads, cut, out)


def solution(mesh):
    rows = P(("grp", "blk", "head"), None)
    return jax.shard_map(
        shards,
        mesh=mesh,
        in_specs=(rows, rows, rows, P("grp"), P("grp")),
        out_specs=rows,
        check_vma=False,
    )
```

```python
import functools
import math

import jax
import jax.numpy as jnp
from jax import lax
from jax.experimental import pallas as pl
from jax.experimental.pallas import tpu as pltpu
from jax.sharding import PartitionSpec as P

HD = 128
CORES = 2
HEADS_PER_TILE = 2
SPLIT = (4, 8)
EXP2_SCALE = math.log2(math.e) / math.sqrt(HD)
LEAST_TOTAL, MOST_TOTAL = 1e-20, 1e30


def matmul_nt(a, b):
    return lax.dot_general(a, b, (((1,), (1,)), ((), ())), preferred_element_type=jnp.float32)


class Place:
    def __init__(self, sizes, info):
        self.prompt_count, self.chips, self.ring, self.tokens = sizes
        self.blocks, self.slots = self.chips * CORES, self.prompt_count + 1
        self.info = info

    def source(self, slot):
        return self.info[2 + slot]

    def first_key(self, slot):
        return self.info[2 + self.slots + slot]

    def kept(self):
        offsets = self.info[1] + lax.broadcasted_iota(jnp.int32, (self.tokens, 1), 0)
        return offsets < self.info[0]


def exact(here, query, key, value, out, group):
    slots, tokens, rows = here.prompt_count + 1, here.tokens, here.ring * here.tokens
    key_row = lax.broadcasted_iota(jnp.int32, (tokens, rows), 1)
    newest_own = rows - tokens + lax.broadcasted_iota(jnp.int32, (tokens, rows), 0)

    def one_head(head, carry):
        columns = pl.ds(pl.multiple_of(head * HD, HD), HD)
        query_one = query[:, columns]

        def part(ref, slot):
            return ref[pl.ds(pl.multiple_of(slot * rows, rows), rows), :]

        def score(slot):
            newest = jnp.where(slot == here.prompt_count, newest_own, rows)
            seen = (key_row >= here.first_key(slot)) & (key_row <= newest)
            return jnp.where(seen, matmul_nt(query_one, part(key, slot)), -jnp.inf)

        row_max = lax.fori_loop(
            0,
            slots,
            lambda j, best: jnp.maximum(best, jnp.max(score(j), axis=1, keepdims=True)),
            jnp.full((tokens, 1), -jnp.inf, jnp.float32),
        )

        def add(slot, carry):
            total, summed = carry
            weights = jnp.exp2((score(slot) - row_max) * EXP2_SCALE)
            total += jnp.sum(weights, axis=1, keepdims=True)
            weights = weights.astype(jnp.bfloat16)
            return total, summed + jnp.dot(weights, part(value, slot), preferred_element_type=jnp.float32)

        zeros = jnp.zeros((tokens, 1), jnp.float32), jnp.zeros((tokens, HD), jnp.float32)
        total, summed = lax.fori_loop(0, slots, add, zeros)
        out[:, columns] = jnp.where(here.kept(), summed / total, 0.0).astype(out.dtype)
        return carry

    lax.fori_loop(0, group, one_head, 0)


def attend_kernel(sizes, where, groups, info, query, *refs):
    prompt_count, chips, ring, tokens = sizes
    here = Place(sizes, info)
    arrays, (out, held, ones, bias, sems) = refs[:-5], refs[-5:]
    kv_head = pl.program_id(0)
    group = query.shape[1] // HD
    masked = bias.shape[1]

    def at(slot, hop):
        return pl.ds(pl.multiple_of((slot * ring + ring - 1 - hop) * tokens, tokens), tokens)

    def seen(slot, hop):
        return (ring - 1 - hop) * tokens >= here.first_key(slot)

    def fetch_of(index, source, slot, hop):
        chunk, low, high, first = groups[index]
        array, column = where[chunk, source, hop]
        return pltpu.make_async_copy(
            arrays[array].at[:, (column + low) * 2 * HD : (column + high) * 2 * HD],
            held.at[at(slot, hop), first * 2 * HD : (first + high - low) * 2 * HD],
            sems.at[index, slot, hop],
        )

    @pl.when(kv_head == 0)
    def _():
        for index in range(len(groups)):

            def fetch(slot, carry):
                wanted = here.source(slot)
                for source in range(here.blocks):

                    @pl.when(wanted == source)
                    def _():
                        for hop in range(ring):

                            @pl.when(seen(slot, hop))
                            def _():
                                fetch_of(index, source, slot, hop).start()

                return carry

            lax.fori_loop(0, here.slots, fetch, 0)

        def fill(slot, carry):
            for hop in range(ring):
                count = jnp.where(seen(slot, hop), 1.0, 0.0)
                ones[at(slot, hop)] = jnp.full((tokens, HD), count, jnp.float32).astype(ones.dtype)

                @pl.when(jnp.logical_not(seen(slot, hop)))
                def _():
                    held[at(slot, hop)] = jnp.zeros((tokens, held.shape[1]), held.dtype)

            return carry

        lax.fori_loop(0, here.slots, fill, 0)
        own = lax.broadcasted_iota(jnp.int32, (tokens, masked), 0)
        key = lax.broadcasted_iota(jnp.int32, (tokens, masked), 1) - (masked - tokens)
        bias[...] = jnp.where(key <= own, 0.0, -jnp.inf)

    for index, (_, _, _, first) in enumerate(groups):

        @pl.when(kv_head == first)
        def _():
            def finish(slot, carry):
                for hop in range(ring):

                    @pl.when(seen(slot, hop))
                    def _():
                        fetch_of(index, 0, slot, hop).wait()

                return carry

            lax.fori_loop(0, here.slots, finish, 0)

    key = held.at[:, pl.ds(pl.multiple_of(kv_head * 2 * HD, 2 * HD), HD)]
    value = held.at[:, pl.ds(pl.multiple_of(kv_head * 2 * HD + HD, HD), HD)]
    keys, values = key[...], jnp.concatenate([value[...], ones[...]], axis=1)
    kept = here.kept()
    least = jnp.full((tokens, HD), jnp.inf, jnp.float32)
    most = jnp.zeros((tokens, HD), jnp.float32)
    for tile in range(group // HEADS_PER_TILE):
        heads = range(tile * HEADS_PER_TILE, (tile + 1) * HEADS_PER_TILE)
        query_tile = jnp.concatenate([query[:, h * HD : (h + 1) * HD] for h in heads], axis=0)
        scores = matmul_nt(query_tile, keys) * EXP2_SCALE
        split = scores.shape[1] - masked
        tail = scores[:, split:].reshape(HEADS_PER_TILE, tokens, masked) + bias[...][None]
        tail = tail.reshape(HEADS_PER_TILE * tokens, masked)
        scores = tail if split == 0 else jnp.concatenate([scores[:, :split], tail], axis=1)
        weights = jnp.exp2(scores).astype(jnp.bfloat16)
        summed = jnp.dot(weights, values, preferred_element_type=jnp.float32)
        for i, h in enumerate(heads):
            part = summed[i * tokens : (i + 1) * tokens]
            total = part[:, HD:]
            least, most = jnp.minimum(least, total), jnp.maximum(most, total)
            out[:, h * HD : (h + 1) * HD] = jnp.where(kept, part[:, :HD] / total, 0.0).astype(out.dtype)
    safe = (jnp.min(least) > LEAST_TOTAL) & (jnp.max(most) < MOST_TOTAL)

    @pl.when(jnp.logical_not(safe))
    def _():
        exact(here, query, key, value, out, group)


def attend(info, query_rows, arrays, where, groups, sizes, kv_heads):
    prompt_count, chips, ring, tokens = sizes
    slots = prompt_count + 1
    group = query_rows.shape[1] // HD // kv_heads
    own_spec = pl.BlockSpec((tokens, group * HD), lambda g, *_: (0, g))
    whole = pl.BlockSpec(memory_space=pl.ANY)
    keys = slots * ring * tokens
    masked = tokens if tokens % HD == 0 else keys
    work = tokens * group * kv_heads * keys
    return pl.pallas_call(
        functools.partial(attend_kernel, sizes, where, groups),
        grid_spec=pltpu.PrefetchScalarGridSpec(
            num_scalar_prefetch=1,
            grid=(kv_heads,),
            in_specs=[own_spec] + [whole] * len(arrays),
            out_specs=own_spec,
            scratch_shapes=[
                pltpu.VMEM((keys, kv_heads * 2 * HD), jnp.bfloat16),
                pltpu.VMEM((keys, HD), jnp.bfloat16),
                pltpu.VMEM((tokens, masked), jnp.float32),
                pltpu.SemaphoreType.DMA((len(groups), slots, ring)),
            ],
        ),
        out_shape=jax.ShapeDtypeStruct(query_rows.shape, query_rows.dtype),
        cost_estimate=pl.CostEstimate(flops=6 * work * HD, bytes_accessed=12 << 20, transcendentals=work),
        compiler_params=pltpu.CompilerParams(vmem_limit_bytes=40 << 20),
    )(info, pltpu.with_memory_space_constraint(query_rows, pltpu.HBM), *arrays)


def pack_kernel(first, end, key, value, out, sems):
    copies = []
    for h in range(first, end):
        for i, x in enumerate((key, value)):
            place = 2 * (h - first) + i
            column = out.at[:, place * HD : (place + 1) * HD]
            copies.append(pltpu.make_async_copy(x.at[:, h * HD : (h + 1) * HD], column, sems.at[place]))
    for copy in copies:
        copy.start()
    for copy in copies:
        copy.wait()


def pack(key_rows, value_rows, first, end):
    whole = pl.BlockSpec(memory_space=pl.ANY)
    count = 2 * (end - first)
    return pl.pallas_call(
        functools.partial(pack_kernel, first, end),
        in_specs=[whole, whole],
        out_specs=whole,
        scratch_shapes=[pltpu.SemaphoreType.DMA((count,))],
        out_shape=jax.ShapeDtypeStruct((key_rows.shape[0], count * HD), key_rows.dtype),
        cost_estimate=pl.CostEstimate(flops=0, bytes_accessed=1 << 19, transcendentals=0),
    )(key_rows, value_rows)


def after(x, *others):
    return lax.optimization_barrier((x, *others))[0]


def scalars(placement, lengths, sizes):
    prompt_count, chips, ring, tokens = sizes
    blocks = chips * CORES
    index, head = lax.axis_index("blk"), lax.axis_index("head")
    block = jnp.sum(jnp.where(jnp.arange(blocks) == index, placement, 0))
    length = jnp.sum(jnp.where(jnp.arange(prompt_count) == block - prompt_count, lengths, 0))
    keep = jnp.where(block >= prompt_count, length, ring * tokens)
    prompt = jnp.arange(prompt_count)
    found = jnp.sum(jnp.where(placement[None, :] == prompt[:, None], jnp.arange(blocks)[None, :], 0), axis=1)
    source = (index // CORES - found // CORES) % chips * CORES + (index + found) % CORES
    first_key = jnp.where(block > prompt, 0, ring * tokens)
    parts = [keep[None], (head * tokens)[None], source, jnp.zeros((1,), jnp.int32), first_key]
    return jnp.concatenate([x.astype(jnp.int32) for x in parts] + [((ring - 1 - head) * tokens)[None]])


def shards(query_rows, key_rows, value_rows, placement, lengths):
    blocks, ring = lax.axis_size("blk"), lax.axis_size("head")
    chips = blocks // CORES
    sizes = (blocks // 2, chips, ring, query_rows.shape[0])
    kv_heads = key_rows.shape[1] // HD
    cut = kv_heads * SPLIT[0] // SPLIT[1]

    def next_hop(x):
        return lax.ppermute(x, "head", [(i, (i + 1) % ring) for i in range(ring)])

    def next_chip(x):
        return lax.ppermute(x, "blk", [(i, (i + CORES) % blocks) for i in range(blocks)])

    def other_core(x):
        return lax.ppermute(x, "blk", [(i, i ^ 1) for i in range(blocks)])

    bounds = (0, cut, kv_heads)
    owns = [pack(key_rows, value_rows, bounds[c], bounds[c + 1]) for c in range(2)]
    info = scalars(*lax.optimization_barrier((placement, lengths, owns[1]))[:2], sizes)
    columns, acrosses = [[x] for x in owns], [[] for _ in owns]
    for hop in range(ring):
        for c in range(2):
            column, across = columns[c], acrosses[c]
            x = column[hop]
            if hop > 0:
                x = after(x, across[hop - 1], *([info] if hop == 1 else []))
            if hop < ring - 1:
                column.append(next_hop(x))
            if hop < ring - 1 or c == 0:
                across.append(next_chip(x))
            else:
                across.append(next_hop(after(across[-1], x)))
    planes = [columns, acrosses]
    bundles = [[(0, c, hop) for c in range(2)] + [(1, c, hop - 1) for c in range(2) if hop] for hop in range(ring)]
    bundles.append([(1, c, ring - 1) for c in range(2)])
    for back in range(2, chips):
        planes.append([[next_chip(x) for x in part] for part in planes[-1]])
        bundles.append([(back, c, hop) for hop in range(ring) for c in range(2)])
    arrays, where = [], {}
    for back, plane in enumerate(planes):
        for c in range(2):
            for hop in range(ring):
                where[c, back * CORES, hop] = len(arrays), 0
                arrays.append(plane[c][hop])
    for bundle in bundles:
        column = 0
        for back, c, hop in bundle:
            where[c, back * CORES + 1, hop] = len(arrays), column
            column += bounds[c + 1] - bounds[c]
        arrays.append(other_core(jnp.concatenate([planes[back][c][hop] for back, c, hop in bundle], axis=1)))
    groups = [(0, 0, 1, 0), (0, 1, cut, 1), (1, 0, kv_heads - cut, cut)]
    return attend(info, query_rows, arrays, where, groups, sizes, kv_heads)


def solution(mesh):
    rows = P(("grp", "blk", "head"), None)
    return jax.shard_map(
        shards,
        mesh=mesh,
        in_specs=(rows, rows, rows, P("grp"), P("grp")),
        out_specs=rows,
        check_vma=False,
    )
```

```python
import functools
import math

import jax
import jax.numpy as jnp
from jax import lax
from jax.experimental import pallas as pl
from jax.experimental.pallas import tpu as pltpu
from jax.sharding import PartitionSpec as P

HD = 128
CORES = 2
HEADS_PER_TILE = 2
SPLIT = (4, 8)
EXP2_SCALE = math.log2(math.e) / math.sqrt(HD)
LEAST_TOTAL, MOST_TOTAL = 1e-20, 1e30


def matmul_nt(a, b):
    return lax.dot_general(a, b, (((1,), (1,)), ((), ())), preferred_element_type=jnp.float32)


class Place:
    def __init__(self, sizes, info):
        self.prompt_count, self.chips, self.ring, self.tokens = sizes
        self.blocks, self.slots = self.chips * CORES, self.prompt_count + 1
        self.info = info

    def source(self, slot):
        return self.info[2 + slot]

    def first_key(self, slot):
        return self.info[2 + self.slots + slot]

    def kept(self):
        offsets = self.info[1] + lax.broadcasted_iota(jnp.int32, (self.tokens, 1), 0)
        return offsets < self.info[0]


def exact(here, query, key, value, out, group):
    slots, tokens, rows = here.prompt_count + 1, here.tokens, here.ring * here.tokens
    key_row = lax.broadcasted_iota(jnp.int32, (tokens, rows), 1)
    newest_own = rows - tokens + lax.broadcasted_iota(jnp.int32, (tokens, rows), 0)

    def one_head(head, carry):
        columns = pl.ds(pl.multiple_of(head * HD, HD), HD)
        query_one = query[:, columns]

        def part(ref, slot):
            return ref[pl.ds(pl.multiple_of(slot * rows, rows), rows), :]

        def score(slot):
            newest = jnp.where(slot == here.prompt_count, newest_own, rows)
            seen = (key_row >= here.first_key(slot)) & (key_row <= newest)
            return jnp.where(seen, matmul_nt(query_one, part(key, slot)), -jnp.inf)

        row_max = lax.fori_loop(
            0,
            slots,
            lambda j, best: jnp.maximum(best, jnp.max(score(j), axis=1, keepdims=True)),
            jnp.full((tokens, 1), -jnp.inf, jnp.float32),
        )

        def add(slot, carry):
            total, summed = carry
            weights = jnp.exp2((score(slot) - row_max) * EXP2_SCALE)
            total += jnp.sum(weights, axis=1, keepdims=True)
            weights = weights.astype(jnp.bfloat16)
            return total, summed + jnp.dot(weights, part(value, slot), preferred_element_type=jnp.float32)

        zeros = jnp.zeros((tokens, 1), jnp.float32), jnp.zeros((tokens, HD), jnp.float32)
        total, summed = lax.fori_loop(0, slots, add, zeros)
        out[:, columns] = jnp.where(here.kept(), summed / total, 0.0).astype(out.dtype)
        return carry

    lax.fori_loop(0, group, one_head, 0)


def attend_kernel(sizes, where, groups, info, query, *refs):
    prompt_count, chips, ring, tokens = sizes
    here = Place(sizes, info)
    arrays, (out, held, ones, bias, sems) = refs[:-5], refs[-5:]
    kv_head = pl.program_id(0)
    group = query.shape[1] // HD
    masked = bias.shape[1]

    def at(slot, hop):
        return pl.ds(pl.multiple_of((slot * ring + ring - 1 - hop) * tokens, tokens), tokens)

    def seen(slot, hop):
        return (ring - 1 - hop) * tokens >= here.first_key(slot)

    def fetch_of(index, source, slot, hop):
        chunk, low, high, first = groups[index]
        array, column = where[chunk, source, hop]
        return pltpu.make_async_copy(
            arrays[array].at[:, (column + low) * 2 * HD : (column + high) * 2 * HD],
            held.at[at(slot, hop), first * 2 * HD : (first + high - low) * 2 * HD],
            sems.at[index, slot, hop],
        )

    @pl.when(kv_head == 0)
    def _():
        for index in range(len(groups)):

            def fetch(slot, carry):
                wanted = here.source(slot)
                for source in range(here.blocks):

                    @pl.when(wanted == source)
                    def _():
                        for hop in range(ring):

                            @pl.when(seen(slot, hop))
                            def _():
                                fetch_of(index, source, slot, hop).start()

                return carry

            lax.fori_loop(0, here.slots, fetch, 0)

        def fill(slot, carry):
            for hop in range(ring):
                count = jnp.where(seen(slot, hop), 1.0, 0.0)
                ones[at(slot, hop)] = jnp.full((tokens, HD), count, jnp.float32).astype(ones.dtype)

                @pl.when(jnp.logical_not(seen(slot, hop)))
                def _():
                    held[at(slot, hop)] = jnp.zeros((tokens, held.shape[1]), held.dtype)

            return carry

        lax.fori_loop(0, here.slots, fill, 0)
        own = lax.broadcasted_iota(jnp.int32, (tokens, masked), 0)
        key = lax.broadcasted_iota(jnp.int32, (tokens, masked), 1) - (masked - tokens)
        bias[...] = jnp.where(key <= own, 0.0, -jnp.inf)

    for index, (_, _, _, first) in enumerate(groups):

        @pl.when(kv_head == first)
        def _():
            def finish(slot, carry):
                for hop in range(ring):

                    @pl.when(seen(slot, hop))
                    def _():
                        fetch_of(index, 0, slot, hop).wait()

                return carry

            lax.fori_loop(0, here.slots, finish, 0)

    key = held.at[:, pl.ds(pl.multiple_of(kv_head * 2 * HD, 2 * HD), HD)]
    value = held.at[:, pl.ds(pl.multiple_of(kv_head * 2 * HD + HD, HD), HD)]
    keys, values = key[...], jnp.concatenate([value[...], ones[...]], axis=1)
    kept = here.kept()
    least = jnp.full((tokens, HD), jnp.inf, jnp.float32)
    most = jnp.zeros((tokens, HD), jnp.float32)
    for tile in range(group // HEADS_PER_TILE):
        heads = range(tile * HEADS_PER_TILE, (tile + 1) * HEADS_PER_TILE)
        query_tile = jnp.concatenate([query[:, h * HD : (h + 1) * HD] for h in heads], axis=0)
        scores = matmul_nt(query_tile, keys) * EXP2_SCALE
        split = scores.shape[1] - masked
        tail = scores[:, split:].reshape(HEADS_PER_TILE, tokens, masked) + bias[...][None]
        tail = tail.reshape(HEADS_PER_TILE * tokens, masked)
        scores = tail if split == 0 else jnp.concatenate([scores[:, :split], tail], axis=1)
        weights = jnp.exp2(scores).astype(jnp.bfloat16)
        summed = jnp.dot(weights, values, preferred_element_type=jnp.float32)
        for i, h in enumerate(heads):
            part = summed[i * tokens : (i + 1) * tokens]
            total = part[:, HD:]
            least, most = jnp.minimum(least, total), jnp.maximum(most, total)
            out[:, h * HD : (h + 1) * HD] = jnp.where(kept, part[:, :HD] / total, 0.0).astype(out.dtype)
    safe = (jnp.min(least) > LEAST_TOTAL) & (jnp.max(most) < MOST_TOTAL)

    @pl.when(jnp.logical_not(safe))
    def _():
        exact(here, query, key, value, out, group)


def attend(info, query_rows, arrays, where, groups, sizes, kv_heads):
    prompt_count, chips, ring, tokens = sizes
    slots = prompt_count + 1
    group = query_rows.shape[1] // HD // kv_heads
    own_spec = pl.BlockSpec((tokens, group * HD), lambda g, *_: (0, g))
    whole = pl.BlockSpec(memory_space=pl.ANY)
    keys = slots * ring * tokens
    masked = tokens if tokens % HD == 0 else keys
    work = tokens * group * kv_heads * keys
    return pl.pallas_call(
        functools.partial(attend_kernel, sizes, where, groups),
        grid_spec=pltpu.PrefetchScalarGridSpec(
            num_scalar_prefetch=1,
            grid=(kv_heads,),
            in_specs=[own_spec] + [whole] * len(arrays),
            out_specs=own_spec,
            scratch_shapes=[
                pltpu.VMEM((keys, kv_heads * 2 * HD), jnp.bfloat16),
                pltpu.VMEM((keys, HD), jnp.bfloat16),
                pltpu.VMEM((tokens, masked), jnp.float32),
                pltpu.SemaphoreType.DMA((len(groups), slots, ring)),
            ],
        ),
        out_shape=jax.ShapeDtypeStruct(query_rows.shape, query_rows.dtype),
        cost_estimate=pl.CostEstimate(flops=6 * work * HD, bytes_accessed=12 << 20, transcendentals=work),
        compiler_params=pltpu.CompilerParams(vmem_limit_bytes=2 * keys * kv_heads * 2 * HD * 2),
    )(info, pltpu.with_memory_space_constraint(query_rows, pltpu.HBM), *arrays)


def pack_kernel(first, end, key, value, out, sems):
    copies = []
    for h in range(first, end):
        for i, x in enumerate((key, value)):
            place = 2 * (h - first) + i
            column = out.at[:, place * HD : (place + 1) * HD]
            copies.append(pltpu.make_async_copy(x.at[:, h * HD : (h + 1) * HD], column, sems.at[place]))
    for copy in copies:
        copy.start()
    for copy in copies:
        copy.wait()


def pack(key_rows, value_rows, first, end):
    whole = pl.BlockSpec(memory_space=pl.ANY)
    count = 2 * (end - first)
    return pl.pallas_call(
        functools.partial(pack_kernel, first, end),
        in_specs=[whole, whole],
        out_specs=whole,
        scratch_shapes=[pltpu.SemaphoreType.DMA((count,))],
        out_shape=jax.ShapeDtypeStruct((key_rows.shape[0], count * HD), key_rows.dtype),
        cost_estimate=pl.CostEstimate(flops=0, bytes_accessed=1 << 19, transcendentals=0),
        compiler_params=pltpu.CompilerParams(vmem_limit_bytes=1 << 18),
    )(key_rows, value_rows)


def after(x, *others):
    return lax.optimization_barrier((x, *others))[0]


def scalars(placement, lengths, sizes):
    prompt_count, chips, ring, tokens = sizes
    blocks = chips * CORES
    index, head = lax.axis_index("blk"), lax.axis_index("head")
    block = jnp.sum(jnp.where(jnp.arange(blocks) == index, placement, 0))
    length = jnp.sum(jnp.where(jnp.arange(prompt_count) == block - prompt_count, lengths, 0))
    keep = jnp.where(block >= prompt_count, length, ring * tokens)
    prompt = jnp.arange(prompt_count)
    found = jnp.sum(jnp.where(placement[None, :] == prompt[:, None], jnp.arange(blocks)[None, :], 0), axis=1)
    source = (index // CORES - found // CORES) % chips * CORES + (index + found) % CORES
    first_key = jnp.where(block > prompt, 0, ring * tokens)
    parts = [keep[None], (head * tokens)[None], source, jnp.zeros((1,), jnp.int32), first_key]
    return jnp.concatenate([x.astype(jnp.int32) for x in parts] + [((ring - 1 - head) * tokens)[None]])


def shards(query_rows, key_rows, value_rows, placement, lengths):
    blocks, ring = lax.axis_size("blk"), lax.axis_size("head")
    chips = blocks // CORES
    sizes = (blocks // 2, chips, ring, query_rows.shape[0])
    kv_heads = key_rows.shape[1] // HD
    cut = kv_heads * SPLIT[0] // SPLIT[1]

    def next_hop(x):
        return lax.ppermute(x, "head", [(i, (i + 1) % ring) for i in range(ring)])

    def next_chip(x):
        return lax.ppermute(x, "blk", [(i, (i + CORES) % blocks) for i in range(blocks)])

    def other_core(x):
        return lax.ppermute(x, "blk", [(i, i ^ 1) for i in range(blocks)])

    bounds = (0, cut, kv_heads)
    owns = [pack(key_rows, value_rows, bounds[c], bounds[c + 1]) for c in range(2)]
    info = scalars(*lax.optimization_barrier((placement, lengths, owns[1]))[:2], sizes)
    columns, acrosses = [[x] for x in owns], [[] for _ in owns]
    for hop in range(ring):
        for c in range(2):
            column, across = columns[c], acrosses[c]
            x = column[hop]
            if hop > 0:
                x = after(x, across[hop - 1], *([info] if hop == 1 else []))
            if hop < ring - 1:
                column.append(next_hop(x))
            if hop < ring - 1 or c == 0:
                across.append(next_chip(x))
            else:
                across.append(next_hop(after(across[-1], x)))
    planes = [columns, acrosses]
    bundles = [[(0, c, hop) for c in range(2)] + [(1, c, hop - 1) for c in range(2) if hop] for hop in range(ring)]
    bundles.append([(1, c, ring - 1) for c in range(2)])
    for back in range(2, chips):
        planes.append([[next_chip(x) for x in part] for part in planes[-1]])
        bundles.append([(back, c, hop) for hop in range(ring) for c in range(2)])
    arrays, where = [], {}
    for back, plane in enumerate(planes):
        for c in range(2):
            for hop in range(ring):
                where[c, back * CORES, hop] = len(arrays), 0
                arrays.append(plane[c][hop])
    for bundle in bundles:
        column = 0
        for back, c, hop in bundle:
            where[c, back * CORES + 1, hop] = len(arrays), column
            column += bounds[c + 1] - bounds[c]
        arrays.append(other_core(jnp.concatenate([planes[back][c][hop] for back, c, hop in bundle], axis=1)))
    groups = [(0, 0, 1, 0), (0, 1, cut, 1), (1, 0, kv_heads - cut, cut)]
    return attend(info, query_rows, arrays, where, groups, sizes, kv_heads)


def solution(mesh):
    rows = P(("grp", "blk", "head"), None)
    return jax.shard_map(
        shards,
        mesh=mesh,
        in_specs=(rows, rows, rows, P("grp"), P("grp")),
        out_specs=rows,
        check_vma=False,
    )
```

```python
import functools
import math

import jax
import jax.numpy as jnp
from jax import lax
from jax.experimental import pallas as pl
from jax.experimental.pallas import tpu as pltpu
from jax.sharding import PartitionSpec as P

HD = 128
CORES = 2
HEADS_PER_TILE = 2
EXP2_SCALE = math.log2(math.e) / math.sqrt(HD)
LEAST_TOTAL, MOST_TOTAL = 1e-20, 1e30


def matmul_nt(a, b):
    return lax.dot_general(a, b, (((1,), (1,)), ((), ())), preferred_element_type=jnp.float32)


class Place:
    def __init__(self, sizes, placement, lengths):
        self.prompt_count, self.chips, self.ring, self.tokens = sizes
        self.blocks, self.slots = self.chips * CORES, self.prompt_count + 1
        self.index, self.head = lax.axis_index("blk"), lax.axis_index("head")
        self.placement, self.lengths = placement, lengths
        self.block = placement[self.index]

    def source(self, slot):
        found = self.index
        for b in range(self.blocks):
            found = jnp.where(self.placement[b] == slot, b, found)
        found = jnp.where(slot == self.prompt_count, self.index, found)
        back = lax.shift_right_logical(self.index, 1) - lax.shift_right_logical(found, 1)
        return jnp.where(back < 0, back + self.chips, back) * CORES + ((self.index ^ found) & 1)

    def first_key(self, slot):
        own = (self.ring - 1 - self.head) * self.tokens
        return jnp.where(slot == self.prompt_count, own, jnp.where(self.block > slot, 0, self.ring * self.tokens))

    def kept(self):
        keep = jnp.int32(self.ring * self.tokens)
        for response in range(self.prompt_count):
            keep = jnp.where(self.block == self.prompt_count + response, self.lengths[response], keep)
        offsets = self.head * self.tokens + lax.broadcasted_iota(jnp.int32, (self.tokens, 1), 0)
        return offsets < keep


def exact(here, query, key, value, out, group):
    slots, tokens, rows = here.prompt_count + 1, here.tokens, here.ring * here.tokens
    key_row = lax.broadcasted_iota(jnp.int32, (tokens, rows), 1)
    newest_own = rows - tokens + lax.broadcasted_iota(jnp.int32, (tokens, rows), 0)

    def one_head(head, carry):
        columns = pl.ds(pl.multiple_of(head * HD, HD), HD)
        query_one = query[:, columns]

        def part(ref, slot):
            return ref[pl.ds(pl.multiple_of(slot * rows, rows), rows), :]

        def score(slot):
            newest = jnp.where(slot == here.prompt_count, newest_own, rows)
            seen = (key_row >= here.first_key(slot)) & (key_row <= newest)
            return jnp.where(seen, matmul_nt(query_one, part(key, slot)), -jnp.inf)

        row_max = lax.fori_loop(
            0,
            slots,
            lambda j, best: jnp.maximum(best, jnp.max(score(j), axis=1, keepdims=True)),
            jnp.full((tokens, 1), -jnp.inf, jnp.float32),
        )

        def add(slot, carry):
            total, summed = carry
            weights = jnp.exp2((score(slot) - row_max) * EXP2_SCALE)
            total += jnp.sum(weights, axis=1, keepdims=True)
            weights = weights.astype(jnp.bfloat16)
            return total, summed + jnp.dot(weights, part(value, slot), preferred_element_type=jnp.float32)

        zeros = jnp.zeros((tokens, 1), jnp.float32), jnp.zeros((tokens, HD), jnp.float32)
        total, summed = lax.fori_loop(0, slots, add, zeros)
        out[:, columns] = jnp.where(here.kept(), summed / total, 0.0).astype(out.dtype)
        return carry

    lax.fori_loop(0, group, one_head, 0)


def attend_kernel(sizes, where, groups, placement, lengths, query, *refs):
    prompt_count, chips, ring, tokens = sizes
    here = Place(sizes, placement, lengths)
    arrays, (out, held_key, held_value, ones, bias, sems) = refs[:-6], refs[-6:]
    kv_head = pl.program_id(0)
    group = query.shape[1] // HD
    masked = bias.shape[1]

    def at(slot, hop):
        return pl.ds(pl.multiple_of((slot * ring + ring - 1 - hop) * tokens, tokens), tokens)

    def seen(slot, hop):
        return (ring - 1 - hop) * tokens >= here.first_key(slot)

    def fetch_of(index, kind, source, slot, hop):
        low, high = groups[index]
        array, column = where[kind, source, hop]
        return pltpu.make_async_copy(
            arrays[array].at[:, column + low * HD : column + high * HD],
            (held_key, held_value)[kind].at[at(slot, hop), low * HD : high * HD],
            sems.at[index, kind, slot, hop],
        )

    @pl.when(kv_head == 0)
    def _():
        for index in range(len(groups)):

            def fetch(slot, carry):
                wanted = here.source(slot)
                for source in range(here.blocks):

                    @pl.when(wanted == source)
                    def _():
                        for hop in range(ring):

                            @pl.when(seen(slot, hop))
                            def _():
                                for kind in range(2):
                                    fetch_of(index, kind, source, slot, hop).start()

                return carry

            lax.fori_loop(0, here.slots, fetch, 0)

        def fill(slot, carry):
            for hop in range(ring):
                count = jnp.where(seen(slot, hop), 1.0, 0.0)
                ones[at(slot, hop)] = jnp.full((tokens, HD), count, jnp.float32).astype(ones.dtype)

                @pl.when(jnp.logical_not(seen(slot, hop)))
                def _():
                    for held in (held_key, held_value):
                        held[at(slot, hop)] = jnp.zeros((tokens, held.shape[1]), held.dtype)

            return carry

        lax.fori_loop(0, here.slots, fill, 0)
        own = lax.broadcasted_iota(jnp.int32, (tokens, masked), 0)
        key = lax.broadcasted_iota(jnp.int32, (tokens, masked), 1) - (masked - tokens)
        bias[...] = jnp.where(key <= own, 0.0, -jnp.inf)

    for index, (first, _) in enumerate(groups):

        @pl.when(kv_head == first)
        def _():
            def finish(slot, carry):
                for hop in range(ring):

                    @pl.when(seen(slot, hop))
                    def _():
                        for kind in range(2):
                            fetch_of(index, kind, 0, slot, hop).wait()

                return carry

            lax.fori_loop(0, here.slots, finish, 0)

    column = pl.ds(pl.multiple_of(kv_head * HD, HD), HD)
    key, value = held_key.at[:, column], held_value.at[:, column]
    kept = here.kept()
    span = HEADS_PER_TILE * HD

    def one_tile(tile, carry):
        least, most = carry
        columns = pl.ds(pl.multiple_of(tile * span, span), span)
        query_tile = query[:, columns]
        query_tile = jnp.concatenate([query_tile[:, h * HD : (h + 1) * HD] for h in range(HEADS_PER_TILE)], axis=0)
        scores = matmul_nt(query_tile, key[...]) * EXP2_SCALE
        split = scores.shape[1] - masked
        tail = scores[:, split:].reshape(HEADS_PER_TILE, tokens, masked) + bias[...][None]
        tail = tail.reshape(HEADS_PER_TILE * tokens, masked)
        scores = tail if split == 0 else jnp.concatenate([scores[:, :split], tail], axis=1)
        weights = jnp.exp2(scores).astype(jnp.bfloat16)
        values = jnp.concatenate([value[...], ones[...]], axis=1)
        summed = jnp.dot(weights, values, preferred_element_type=jnp.float32)
        results = []
        for i in range(HEADS_PER_TILE):
            part = summed[i * tokens : (i + 1) * tokens]
            total = part[:, HD:]
            least, most = jnp.minimum(least, total), jnp.maximum(most, total)
            results.append(jnp.where(kept, part[:, :HD] / total, 0.0).astype(out.dtype))
        out[:, columns] = jnp.concatenate(results, axis=1)
        return least, most

    zeros = jnp.zeros((tokens, HD), jnp.float32)
    least, most = lax.fori_loop(0, group // HEADS_PER_TILE, one_tile, (zeros + jnp.inf, zeros))
    safe = (jnp.min(least) > LEAST_TOTAL) & (jnp.max(most) < MOST_TOTAL)

    @pl.when(jnp.logical_not(safe))
    def _():
        exact(here, query, key, value, out, group)


def attend(placement, lengths, query_rows, arrays, where, groups, sizes, kv_heads):
    prompt_count, chips, ring, tokens = sizes
    slots = prompt_count + 1
    group = query_rows.shape[1] // HD // kv_heads
    own_spec = pl.BlockSpec((tokens, group * HD), lambda g, *_: (0, g))
    whole = pl.BlockSpec(memory_space=pl.ANY)
    keys = slots * ring * tokens
    masked = tokens if tokens % HD == 0 else keys
    work = tokens * group * kv_heads * keys
    return pl.pallas_call(
        functools.partial(attend_kernel, sizes, where, groups),
        grid_spec=pltpu.PrefetchScalarGridSpec(
            num_scalar_prefetch=2,
            grid=(kv_heads,),
            in_specs=[own_spec] + [whole] * len(arrays),
            out_specs=own_spec,
            scratch_shapes=[
                pltpu.VMEM((keys, kv_heads * HD), jnp.bfloat16),
                pltpu.VMEM((keys, kv_heads * HD), jnp.bfloat16),
                pltpu.VMEM((keys, HD), jnp.bfloat16),
                pltpu.VMEM((tokens, masked), jnp.float32),
                pltpu.SemaphoreType.DMA((len(groups), 2, slots, ring)),
            ],
        ),
        out_shape=jax.ShapeDtypeStruct(query_rows.shape, query_rows.dtype),
        cost_estimate=pl.CostEstimate(flops=6 * work * HD, bytes_accessed=12 << 20, transcendentals=work),
        compiler_params=pltpu.CompilerParams(vmem_limit_bytes=2 * keys * kv_heads * 2 * HD * 2),
    )(placement, lengths, pltpu.with_memory_space_constraint(query_rows, pltpu.HBM), *arrays)


def after(x, *others):
    return lax.optimization_barrier((x, *others))[0]


def shards(query_rows, key_rows, value_rows, placement, lengths):
    blocks, ring = lax.axis_size("blk"), lax.axis_size("head")
    chips = blocks // CORES
    sizes = (blocks // 2, chips, ring, query_rows.shape[0])
    width = key_rows.shape[1]
    kv_heads = width // HD

    def next_hop(x):
        return lax.ppermute(x, "head", [(i, (i + 1) % ring) for i in range(ring)])

    def next_chip(x):
        return lax.ppermute(x, "blk", [(i, (i + CORES) % blocks) for i in range(blocks)])

    def other_core(x):
        return lax.ppermute(x, "blk", [(i, i ^ 1) for i in range(blocks)])

    columns, acrosses = [[key_rows], [value_rows]], [[], []]
    for hop in range(ring):
        for c in range(2):
            column, across = columns[c], acrosses[c]
            x = column[hop]
            if hop > 0:
                x = after(x, across[hop - 1])
            if hop < ring - 1:
                column.append(next_hop(x))
            if hop < ring - 1 or c == 1:
                across.append(next_chip(x))
            else:
                across.append(next_hop(after(across[-1], x)))
    planes = [columns, acrosses]
    bundles = [[(0, c, hop) for c in range(2)] + [(1, c, hop - 1) for c in range(2) if hop] for hop in range(ring - 1)]
    bundles += [[(0, c, ring - 1), (1, c, ring - 2)] for c in range(2)] + [[(1, c, ring - 1)] for c in range(2)]
    for back in range(2, chips):
        planes.append([[next_chip(x) for x in part] for part in planes[-1]])
        bundles.append([(back, c, hop) for hop in range(ring) for c in range(2)])
    arrays, where = [], {}
    for back, plane in enumerate(planes):
        for c in range(2):
            for hop in range(ring):
                where[c, back * CORES, hop] = len(arrays), 0
                arrays.append(plane[c][hop])
    for bundle in bundles:
        for place, (back, c, hop) in enumerate(bundle):
            where[c, back * CORES + 1, hop] = len(arrays), place * width
        packed = jnp.concatenate([planes[back][c][hop] for back, c, hop in bundle], axis=1)
        for c in range(2):
            if bundle == bundles[ring - 1 + c]:
                packed = after(packed, planes[1][c][ring - 1])
        if bundle == bundles[ring + 2]:
            packed = after(packed, arrays[-1])
        arrays.append(other_core(packed))
    groups = [(0, 1), (1, kv_heads)]
    return attend(placement, lengths, query_rows, arrays, where, groups, sizes, kv_heads)


def solution(mesh):
    rows = P(("grp", "blk", "head"), None)
    return jax.shard_map(
        shards,
        mesh=mesh,
        in_specs=(rows, rows, rows, P("grp"), P("grp")),
        out_specs=rows,
        check_vma=False,
    )
```

```python
import functools
import math

import jax
import jax.numpy as jnp
from jax import lax
from jax.experimental import pallas as pl
from jax.experimental.pallas import tpu as pltpu
from jax.sharding import PartitionSpec as P

HD = 128
CORES = 2
HEADS_PER_TILE = 8
EXP2_SCALE = math.log2(math.e) / math.sqrt(HD)
LEAST_TOTAL, MOST_TOTAL = 1e-20, 1e30


def matmul_nt(a, b):
    return lax.dot_general(a, b, (((1,), (1,)), ((), ())), preferred_element_type=jnp.float32)


class Place:
    def __init__(self, sizes, placement, lengths):
        self.prompt_count, self.chips, self.ring, self.tokens = sizes
        self.blocks, self.slots = self.chips * CORES, self.prompt_count + 1
        self.index, self.head = lax.axis_index("blk"), lax.axis_index("head")
        self.placement, self.lengths = placement, lengths
        self.block = placement[self.index]

    def source(self, slot):
        found = self.index
        for b in range(self.blocks):
            found = jnp.where(self.placement[b] == slot, b, found)
        found = jnp.where(slot == self.prompt_count, self.index, found)
        back = lax.shift_right_logical(self.index, 1) - lax.shift_right_logical(found, 1)
        return jnp.where(back < 0, back + self.chips, back) * CORES + ((self.index ^ found) & 1)

    def first_key(self, slot):
        own = (self.ring - 1 - self.head) * self.tokens
        return jnp.where(slot == self.prompt_count, own, jnp.where(self.block > slot, 0, self.ring * self.tokens))

    def kept(self):
        keep = jnp.int32(self.ring * self.tokens)
        for response in range(self.prompt_count):
            keep = jnp.where(self.block == self.prompt_count + response, self.lengths[response], keep)
        offsets = self.head * self.tokens + lax.broadcasted_iota(jnp.int32, (self.tokens, 1), 0)
        return offsets < keep


def exact(here, query, key, value, out, group):
    slots, tokens, rows = here.prompt_count + 1, here.tokens, here.ring * here.tokens
    key_row = lax.broadcasted_iota(jnp.int32, (tokens, rows), 1)
    newest_own = rows - tokens + lax.broadcasted_iota(jnp.int32, (tokens, rows), 0)

    def one_head(head, carry):
        columns = pl.ds(pl.multiple_of(head * HD, HD), HD)
        query_one = query[:, columns]

        def part(ref, slot):
            return ref[pl.ds(pl.multiple_of(slot * rows, rows), rows), :]

        def score(slot):
            newest = jnp.where(slot == here.prompt_count, newest_own, rows)
            seen = (key_row >= here.first_key(slot)) & (key_row <= newest)
            return jnp.where(seen, matmul_nt(query_one, part(key, slot)), -jnp.inf)

        row_max = lax.fori_loop(
            0,
            slots,
            lambda j, best: jnp.maximum(best, jnp.max(score(j), axis=1, keepdims=True)),
            jnp.full((tokens, 1), -jnp.inf, jnp.float32),
        )

        def add(slot, carry):
            total, summed = carry
            weights = jnp.exp2((score(slot) - row_max) * EXP2_SCALE)
            total += jnp.sum(weights, axis=1, keepdims=True)
            weights = weights.astype(jnp.bfloat16)
            return total, summed + jnp.dot(weights, part(value, slot), preferred_element_type=jnp.float32)

        zeros = jnp.zeros((tokens, 1), jnp.float32), jnp.zeros((tokens, HD), jnp.float32)
        total, summed = lax.fori_loop(0, slots, add, zeros)
        out[:, columns] = jnp.where(here.kept(), summed / total, 0.0).astype(out.dtype)
        return carry

    lax.fori_loop(0, group, one_head, 0)


def attend_kernel(sizes, where, groups, placement, lengths, query, *refs):
    prompt_count, chips, ring, tokens = sizes
    here = Place(sizes, placement, lengths)
    arrays, (out, held_key, held_value, ones, bias, sems) = refs[:-6], refs[-6:]
    kv_head = pl.program_id(0)
    group = query.shape[1] // HD
    masked = bias.shape[1]

    def at(slot, hop):
        return pl.ds(pl.multiple_of((slot * ring + ring - 1 - hop) * tokens, tokens), tokens)

    def seen(slot, hop):
        return (ring - 1 - hop) * tokens >= here.first_key(slot)

    def fetch_of(index, kind, source, slot, hop):
        low, high = groups[index]
        array, column = where[kind, source, hop]
        return pltpu.make_async_copy(
            arrays[array].at[:, column + low * HD : column + high * HD],
            (held_key, held_value)[kind].at[at(slot, hop), low * HD : high * HD],
            sems.at[index, kind, slot, hop],
        )

    @pl.when(kv_head == 0)
    def _():
        for index in range(len(groups)):

            def fetch(slot, carry):
                wanted = here.source(slot)
                for source in range(here.blocks):

                    @pl.when(wanted == source)
                    def _():
                        for hop in range(ring):

                            @pl.when(seen(slot, hop))
                            def _():
                                for kind in range(2):
                                    fetch_of(index, kind, source, slot, hop).start()

                return carry

            lax.fori_loop(0, here.slots, fetch, 0)

        def fill(slot, carry):
            for hop in range(ring):
                count = jnp.where(seen(slot, hop), 1.0, 0.0)
                ones[at(slot, hop)] = jnp.full((tokens, HD), count, jnp.float32).astype(ones.dtype)

                @pl.when(jnp.logical_not(seen(slot, hop)))
                def _():
                    for held in (held_key, held_value):
                        held[at(slot, hop)] = jnp.zeros((tokens, held.shape[1]), held.dtype)

            return carry

        lax.fori_loop(0, here.slots, fill, 0)
        own = lax.broadcasted_iota(jnp.int32, (tokens, masked), 0)
        key = lax.broadcasted_iota(jnp.int32, (tokens, masked), 1) - (masked - tokens)
        bias[...] = jnp.where(key <= own, 0.0, -jnp.inf)

    for index, (first, _) in enumerate(groups):

        @pl.when(kv_head == first)
        def _():
            def finish(slot, carry):
                for hop in range(ring):

                    @pl.when(seen(slot, hop))
                    def _():
                        for kind in range(2):
                            fetch_of(index, kind, 0, slot, hop).wait()

                return carry

            lax.fori_loop(0, here.slots, finish, 0)

    column = pl.ds(pl.multiple_of(kv_head * HD, HD), HD)
    key, value = held_key.at[:, column], held_value.at[:, column]
    kept = here.kept()
    zeros = jnp.zeros((tokens, HD), jnp.float32)
    least, most = zeros + jnp.inf, zeros
    rows = ring * tokens
    for tile in range(group // HEADS_PER_TILE):
        heads = range(tile * HEADS_PER_TILE, (tile + 1) * HEADS_PER_TILE)
        query_tile = jnp.concatenate([query[:, h * HD : (h + 1) * HD] for h in heads], axis=0)
        summed = None
        for slot in range(here.slots):
            block = pl.ds(slot * rows, rows)
            scores = matmul_nt(query_tile, key[block, :]) * EXP2_SCALE
            if slot == prompt_count:
                split = rows - masked
                tail = scores[:, split:].reshape(HEADS_PER_TILE, tokens, masked) + bias[...][None]
                tail = tail.reshape(HEADS_PER_TILE * tokens, masked)
                scores = tail if split == 0 else jnp.concatenate([scores[:, :split], tail], axis=1)
            weights = jnp.exp2(scores).astype(jnp.bfloat16)
            values = jnp.concatenate([value[block, :], ones[block, :]], axis=1)
            part = jnp.dot(weights, values, preferred_element_type=jnp.float32)
            summed = part if summed is None else summed + part
        for i, h in enumerate(heads):
            part = summed[i * tokens : (i + 1) * tokens]
            total = part[:, HD:]
            least, most = jnp.minimum(least, total), jnp.maximum(most, total)
            out[:, h * HD : (h + 1) * HD] = jnp.where(kept, part[:, :HD] / total, 0.0).astype(out.dtype)
    safe = (jnp.min(least) > LEAST_TOTAL) & (jnp.max(most) < MOST_TOTAL)

    @pl.when(jnp.logical_not(safe))
    def _():
        exact(here, query, key, value, out, group)


def attend(placement, lengths, query_rows, arrays, where, groups, sizes, kv_heads):
    prompt_count, chips, ring, tokens = sizes
    slots = prompt_count + 1
    group = query_rows.shape[1] // HD // kv_heads
    own_spec = pl.BlockSpec((tokens, group * HD), lambda g, *_: (0, g))
    whole = pl.BlockSpec(memory_space=pl.ANY)
    keys = slots * ring * tokens
    masked = tokens if tokens % HD == 0 else ring * tokens
    work = tokens * group * kv_heads * keys
    return pl.pallas_call(
        functools.partial(attend_kernel, sizes, where, groups),
        grid_spec=pltpu.PrefetchScalarGridSpec(
            num_scalar_prefetch=2,
            grid=(kv_heads,),
            in_specs=[own_spec] + [whole] * len(arrays),
            out_specs=own_spec,
            scratch_shapes=[
                pltpu.VMEM((keys, kv_heads * HD), jnp.bfloat16),
                pltpu.VMEM((keys, kv_heads * HD), jnp.bfloat16),
                pltpu.VMEM((keys, HD), jnp.bfloat16),
                pltpu.VMEM((tokens, masked), jnp.float32),
                pltpu.SemaphoreType.DMA((len(groups), 2, slots, ring)),
            ],
        ),
        out_shape=jax.ShapeDtypeStruct(query_rows.shape, query_rows.dtype),
        cost_estimate=pl.CostEstimate(flops=6 * work * HD, bytes_accessed=12 << 20, transcendentals=work),
        compiler_params=pltpu.CompilerParams(vmem_limit_bytes=2 * keys * kv_heads * 2 * HD * 2 + (12 << 20)),
    )(placement, lengths, pltpu.with_memory_space_constraint(query_rows, pltpu.HBM), *arrays)


def after(x, *others):
    return lax.optimization_barrier((x, *others))[0]


def shards(query_rows, key_rows, value_rows, placement, lengths):
    blocks, ring = lax.axis_size("blk"), lax.axis_size("head")
    chips = blocks // CORES
    sizes = (blocks // 2, chips, ring, query_rows.shape[0])
    width = key_rows.shape[1]
    kv_heads = width // HD

    def next_hop(x):
        return lax.ppermute(x, "head", [(i, (i + 1) % ring) for i in range(ring)])

    def next_chip(x):
        return lax.ppermute(x, "blk", [(i, (i + CORES) % blocks) for i in range(blocks)])

    def other_core(x):
        return lax.ppermute(x, "blk", [(i, i ^ 1) for i in range(blocks)])

    columns, acrosses = [[key_rows], [value_rows]], [[], []]
    for hop in range(ring):
        for c in range(2):
            column, across = columns[c], acrosses[c]
            x = column[hop]
            if hop > 0:
                x = after(x, across[hop - 1])
            if hop < ring - 1:
                column.append(next_hop(x))
            if hop < ring - 1 or c == 1:
                across.append(next_chip(x))
            else:
                across.append(next_hop(after(across[-1], x)))
    planes = [columns, acrosses]
    bundles = [[(0, c, hop) for c in range(2)] + [(1, c, hop - 1) for c in range(2) if hop] for hop in range(ring - 1)]
    bundles += [[(0, c, ring - 1), (1, c, ring - 2)] for c in range(2)] + [[(1, c, ring - 1)] for c in range(2)]
    for back in range(2, chips):
        planes.append([[next_chip(x) for x in part] for part in planes[-1]])
        bundles.append([(back, c, hop) for hop in range(ring) for c in range(2)])
    arrays, where = [], {}
    for back, plane in enumerate(planes):
        for c in range(2):
            for hop in range(ring):
                where[c, back * CORES, hop] = len(arrays), 0
                arrays.append(plane[c][hop])
    for bundle in bundles:
        for place, (back, c, hop) in enumerate(bundle):
            where[c, back * CORES + 1, hop] = len(arrays), place * width
        packed = jnp.concatenate([planes[back][c][hop] for back, c, hop in bundle], axis=1)
        for c in range(2):
            if bundle == bundles[ring - 1 + c]:
                packed = after(packed, planes[1][c][ring - 1])
        if bundle == bundles[ring + 2]:
            packed = after(packed, arrays[-1])
        arrays.append(other_core(packed))
    groups = [(0, 1), (1, kv_heads)]
    return attend(placement, lengths, query_rows, arrays, where, groups, sizes, kv_heads)


def solution(mesh):
    rows = P(("grp", "blk", "head"), None)
    return jax.shard_map(
        shards,
        mesh=mesh,
        in_specs=(rows, rows, rows, P("grp"), P("grp")),
        out_specs=rows,
        check_vma=False,
    )
```

```python
import functools
import math

import jax
import jax.numpy as jnp
from jax import lax
from jax.experimental import pallas as pl
from jax.experimental.pallas import tpu as pltpu
from jax.sharding import PartitionSpec as P

HD = 128
CORES = 2
HEADS_PER_TILE = 2
RESIDENT_BYTES = 16 << 20
EXP2_SCALE = math.log2(math.e) / math.sqrt(HD)
LEAST_TOTAL, MOST_TOTAL = 1e-20, 1e30


def matmul_nt(a, b):
    return lax.dot_general(a, b, (((1,), (1,)), ((), ())), preferred_element_type=jnp.float32)


class Place:
    def __init__(self, sizes, placement, lengths):
        self.prompt_count, self.chips, self.ring, self.tokens = sizes
        self.blocks, self.slots = self.chips * CORES, self.prompt_count + 1
        self.index, self.head = lax.axis_index("blk"), lax.axis_index("head")
        self.placement, self.lengths = placement, lengths
        self.block = placement[self.index]

    def source(self, slot):
        found = self.index
        for b in range(self.blocks):
            found = jnp.where(self.placement[b] == slot, b, found)
        found = jnp.where(slot == self.prompt_count, self.index, found)
        back = lax.shift_right_logical(self.index, 1) - lax.shift_right_logical(found, 1)
        return jnp.where(back < 0, back + self.chips, back) * CORES + ((self.index ^ found) & 1)

    def first_key(self, slot):
        own = (self.ring - 1 - self.head) * self.tokens
        return jnp.where(slot == self.prompt_count, own, jnp.where(self.block > slot, 0, self.ring * self.tokens))

    def kept(self):
        keep = jnp.int32(self.ring * self.tokens)
        for response in range(self.prompt_count):
            keep = jnp.where(self.block == self.prompt_count + response, self.lengths[response], keep)
        offsets = self.head * self.tokens + lax.broadcasted_iota(jnp.int32, (self.tokens, 1), 0)
        return offsets < keep


def exact(here, query, key, value, out):
    slots, tokens, rows = here.prompt_count + 1, here.tokens, here.ring * here.tokens
    key_row = lax.broadcasted_iota(jnp.int32, (tokens, rows), 1)
    newest_own = rows - tokens + lax.broadcasted_iota(jnp.int32, (tokens, rows), 0)

    def one_head(head, carry):
        columns = pl.ds(pl.multiple_of(head * HD, HD), HD)
        query_one = query[:, columns]

        def part(ref, slot):
            return ref[pl.ds(pl.multiple_of(slot * rows, rows), rows), :]

        def score(slot):
            newest = jnp.where(slot == here.prompt_count, newest_own, rows)
            seen = (key_row >= here.first_key(slot)) & (key_row <= newest)
            return jnp.where(seen, matmul_nt(query_one, part(key, slot)), -jnp.inf)

        row_max = lax.fori_loop(
            0,
            slots,
            lambda j, best: jnp.maximum(best, jnp.max(score(j), axis=1, keepdims=True)),
            jnp.full((tokens, 1), -jnp.inf, jnp.float32),
        )

        def add(slot, carry):
            total, summed = carry
            weights = jnp.exp2((score(slot) - row_max) * EXP2_SCALE)
            total += jnp.sum(weights, axis=1, keepdims=True)
            weights = weights.astype(jnp.bfloat16)
            return total, summed + jnp.dot(weights, part(value, slot), preferred_element_type=jnp.float32)

        zeros = jnp.zeros((tokens, 1), jnp.float32), jnp.zeros((tokens, HD), jnp.float32)
        total, summed = lax.fori_loop(0, slots, add, zeros)
        out[:, columns] = jnp.where(here.kept(), summed / total, 0.0).astype(out.dtype)
        return carry

    lax.fori_loop(0, query.shape[1] // HD, one_head, 0)


def attend_kernel(sizes, where, resident, placement, lengths, query_all, *refs):
    prompt_count, chips, ring, tokens = sizes
    here = Place(sizes, placement, lengths)
    arrays, refs = refs[:-9], refs[-9:]
    out_all, query_held, out_held, held_key, held_value, ones, bias, sems, fetch_sem = refs
    width = held_key.shape[1]
    kv_heads = width // HD
    span = query_all.shape[1] // kv_heads
    group = span // HD
    masked = bias.shape[1]

    def heads_of(kv_head):
        return pl.ds(pl.multiple_of(kv_head * span, span), span)

    def query_copy(kv_head):
        columns = heads_of(kv_head)
        return pltpu.make_async_copy(query_all.at[:, columns], query_held.at[:, columns], sems.at[0, kv_head])

    def out_copy(kv_head):
        columns = heads_of(kv_head)
        return pltpu.make_async_copy(out_held.at[:, columns], out_all.at[:, columns], sems.at[1, kv_head])

    for kv_head in range(kv_heads):
        query_copy(kv_head).start()

    def take(slot, carry):
        wanted = here.source(slot)
        for hop in range(ring):
            rows = pl.ds(pl.multiple_of((slot * ring + ring - 1 - hop) * tokens, tokens), tokens)
            seen = (ring - 1 - hop) * tokens >= here.first_key(slot)
            count = jnp.where(seen, 1.0, 0.0)
            ones[rows] = jnp.full((tokens, HD), count, jnp.float32).astype(ones.dtype)
            for kind, held in enumerate((held_key, held_value)):

                @pl.when(jnp.logical_not(seen))
                def _():
                    held[rows] = jnp.zeros((tokens, width), held.dtype)

                for source in range(here.blocks):
                    array, column = where[kind, source, hop]

                    @pl.when(seen & (wanted == source))
                    def _():
                        piece = arrays[array].at[:, column : column + width]
                        if resident:
                            held[rows] = piece[...]
                        else:
                            copy = pltpu.make_async_copy(piece, held.at[rows], fetch_sem)
                            copy.start()
                            copy.wait()

        return carry

    lax.fori_loop(0, here.slots, take, 0)
    own = lax.broadcasted_iota(jnp.int32, (tokens, masked), 0)
    key_row = lax.broadcasted_iota(jnp.int32, (tokens, masked), 1) - (masked - tokens)
    bias[...] = jnp.where(key_row <= own, 0.0, -jnp.inf)
    kept = here.kept()

    def of_head(kv_head):
        column = pl.ds(pl.multiple_of(kv_head * HD, HD), HD)
        columns = heads_of(kv_head)
        return query_held.at[:, columns], held_key.at[:, column], held_value.at[:, column], out_held.at[:, columns]

    def one_kv_head(kv_head, carry):
        least, most = carry
        query, key, value, out = of_head(kv_head)
        query_copy(kv_head).wait()
        keys, values = key[...], jnp.concatenate([value[...], ones[...]], axis=1)
        for tile in range(group // HEADS_PER_TILE):
            heads = range(tile * HEADS_PER_TILE, (tile + 1) * HEADS_PER_TILE)
            query_tile = jnp.concatenate([query[:, h * HD : (h + 1) * HD] for h in heads], axis=0)
            scores = matmul_nt(query_tile, keys) * EXP2_SCALE
            split = scores.shape[1] - masked
            tail = scores[:, split:].reshape(HEADS_PER_TILE, tokens, masked) + bias[...][None]
            tail = tail.reshape(HEADS_PER_TILE * tokens, masked)
            scores = tail if split == 0 else jnp.concatenate([scores[:, :split], tail], axis=1)
            weights = jnp.exp2(scores).astype(jnp.bfloat16)
            summed = jnp.dot(weights, values, preferred_element_type=jnp.float32)
            for i, h in enumerate(heads):
                part = summed[i * tokens : (i + 1) * tokens]
                total = part[:, HD:]
                least, most = jnp.minimum(least, total), jnp.maximum(most, total)
                out[:, h * HD : (h + 1) * HD] = jnp.where(kept, part[:, :HD] / total, 0.0).astype(out.dtype)
        out_copy(kv_head).start()
        return least, most

    zeros = jnp.zeros((tokens, HD), jnp.float32)
    least, most = lax.fori_loop(0, kv_heads, one_kv_head, (zeros + jnp.inf, zeros))
    safe = (jnp.min(least) > LEAST_TOTAL) & (jnp.max(most) < MOST_TOTAL)
    for kv_head in range(kv_heads):
        out_copy(kv_head).wait()

    @pl.when(jnp.logical_not(safe))
    def _():
        def again(kv_head, carry):
            query, key, value, out = of_head(kv_head)
            exact(here, query, key, value, out)
            out_copy(kv_head).start()
            out_copy(kv_head).wait()
            return carry

        lax.fori_loop(0, kv_heads, again, 0)


def attend(placement, lengths, query_rows, arrays, where, sizes, kv_heads):
    prompt_count, chips, ring, tokens = sizes
    slots = prompt_count + 1
    width = kv_heads * HD
    keys = slots * ring * tokens
    masked = tokens if tokens % HD == 0 else keys
    work = query_rows.size // HD * keys
    resident = sum(x.size * x.dtype.itemsize for x in arrays) <= RESIDENT_BYTES
    scalar, whole = pl.BlockSpec(memory_space=pltpu.SMEM), pl.BlockSpec(memory_space=pl.ANY)
    piece = pl.BlockSpec(memory_space=pltpu.VMEM) if resident else whole
    return pl.pallas_call(
        functools.partial(attend_kernel, sizes, where, resident),
        in_specs=[scalar, scalar, whole] + [piece] * len(arrays),
        out_specs=whole,
        scratch_shapes=[
            pltpu.VMEM(query_rows.shape, query_rows.dtype),
            pltpu.VMEM(query_rows.shape, query_rows.dtype),
            pltpu.VMEM((keys, width), jnp.bfloat16),
            pltpu.VMEM((keys, width), jnp.bfloat16),
            pltpu.VMEM((keys, HD), jnp.bfloat16),
            pltpu.VMEM((tokens, masked), jnp.float32),
            pltpu.SemaphoreType.DMA((2, kv_heads)),
            pltpu.SemaphoreType.DMA,
        ],
        out_shape=jax.ShapeDtypeStruct(query_rows.shape, query_rows.dtype),
        cost_estimate=pl.CostEstimate(flops=6 * work * HD, bytes_accessed=12 << 20, transcendentals=work),
        compiler_params=pltpu.CompilerParams(vmem_limit_bytes=2 * keys * width * 2 + (14 << 20)),
    )(placement, lengths, pltpu.with_memory_space_constraint(query_rows, pltpu.HBM), *arrays)


def after(x, *others):
    return lax.optimization_barrier((x, *others))[0]


def shards(query_rows, key_rows, value_rows, placement, lengths):
    blocks, ring = lax.axis_size("blk"), lax.axis_size("head")
    chips = blocks // CORES
    sizes = (blocks // 2, chips, ring, query_rows.shape[0])
    width = key_rows.shape[1]
    kv_heads = width // HD

    def next_hop(x):
        return lax.ppermute(x, "head", [(i, (i + 1) % ring) for i in range(ring)])

    def next_chip(x):
        return lax.ppermute(x, "blk", [(i, (i + CORES) % blocks) for i in range(blocks)])

    def other_core(x):
        return lax.ppermute(x, "blk", [(i, i ^ 1) for i in range(blocks)])

    columns, acrosses = [[key_rows], [value_rows]], [[], []]
    for hop in range(ring):
        for c in range(2):
            column, across = columns[c], acrosses[c]
            x = column[hop]
            if hop > 0:
                x = after(x, across[hop - 1])
            if hop < ring - 1:
                column.append(next_hop(x))
            if hop < ring - 1 or c == 1:
                across.append(next_chip(x))
            else:
                across.append(next_hop(after(across[-1], x)))
    planes = [columns, acrosses]
    bundles = [[(0, c, hop) for c in range(2)] + [(1, c, hop - 1) for c in range(2) if hop] for hop in range(ring - 1)]
    bundles += [[(0, c, ring - 1), (1, c, ring - 2)] for c in range(2)] + [[(1, c, ring - 1)] for c in range(2)]
    for back in range(2, chips):
        planes.append([[next_chip(x) for x in part] for part in planes[-1]])
        bundles.append([(back, c, hop) for hop in range(ring) for c in range(2)])
    arrays, where = [], {}
    for back, plane in enumerate(planes):
        for c in range(2):
            for hop in range(ring):
                where[c, back * CORES, hop] = len(arrays), 0
                arrays.append(plane[c][hop])
    for bundle in bundles:
        for place, (back, c, hop) in enumerate(bundle):
            where[c, back * CORES + 1, hop] = len(arrays), place * width
        packed = jnp.concatenate([planes[back][c][hop] for back, c, hop in bundle], axis=1)
        for c in range(2):
            if bundle == bundles[ring - 1 + c]:
                packed = after(packed, planes[1][c][ring - 1])
        if bundle == bundles[ring + 2]:
            packed = after(packed, arrays[-1])
        arrays.append(other_core(packed))
    return attend(placement, lengths, query_rows, arrays, where, sizes, kv_heads)


def solution(mesh):
    rows = P(("grp", "blk", "head"), None)
    return jax.shard_map(
        shards,
        mesh=mesh,
        in_specs=(rows, rows, rows, P("grp"), P("grp")),
        out_specs=rows,
        check_vma=False,
    )
```

```python
import functools
import math

import jax
import jax.numpy as jnp
from jax import lax
from jax.experimental import pallas as pl
from jax.experimental.pallas import tpu as pltpu
from jax.sharding import PartitionSpec as P

HD = 128
CORES = 2
HEADS_PER_TILE = 2
RESIDENT_BYTES = 16 << 20
EXP2_SCALE = math.log2(math.e) / math.sqrt(HD)
LEAST_TOTAL, MOST_TOTAL = 1e-20, 1e30


def matmul_nt(a, b):
    return lax.dot_general(a, b, (((1,), (1,)), ((), ())), preferred_element_type=jnp.float32)


class Place:
    def __init__(self, sizes, placement, lengths):
        self.prompt_count, self.chips, self.ring, self.tokens = sizes
        self.blocks, self.slots = self.chips * CORES, self.prompt_count + 1
        self.index, self.head = lax.axis_index("blk"), lax.axis_index("head")
        self.placement, self.lengths = placement, lengths
        self.block = placement[self.index]

    def source(self, slot):
        found = self.index
        for b in range(self.blocks):
            found = jnp.where(self.placement[b] == slot, b, found)
        found = jnp.where(slot == self.prompt_count, self.index, found)
        back = lax.shift_right_logical(self.index, 1) - lax.shift_right_logical(found, 1)
        return jnp.where(back < 0, back + self.chips, back) * CORES + ((self.index ^ found) & 1)

    def first_key(self, slot):
        own = (self.ring - 1 - self.head) * self.tokens
        return jnp.where(slot == self.prompt_count, own, jnp.where(self.block > slot, 0, self.ring * self.tokens))

    def kept(self):
        keep = jnp.int32(self.ring * self.tokens)
        for response in range(self.prompt_count):
            keep = jnp.where(self.block == self.prompt_count + response, self.lengths[response], keep)
        offsets = self.head * self.tokens + lax.broadcasted_iota(jnp.int32, (self.tokens, 1), 0)
        return offsets < keep


def exact(here, query, key, value, out):
    slots, tokens, rows = here.prompt_count + 1, here.tokens, here.ring * here.tokens
    key_row = lax.broadcasted_iota(jnp.int32, (tokens, rows), 1)
    newest_own = rows - tokens + lax.broadcasted_iota(jnp.int32, (tokens, rows), 0)

    def one_head(head, carry):
        columns = pl.ds(pl.multiple_of(head * HD, HD), HD)
        query_one = query[:, columns]

        def part(ref, slot):
            return ref[pl.ds(pl.multiple_of(slot * rows, rows), rows), :]

        def score(slot):
            newest = jnp.where(slot == here.prompt_count, newest_own, rows)
            seen = (key_row >= here.first_key(slot)) & (key_row <= newest)
            return jnp.where(seen, matmul_nt(query_one, part(key, slot)), -jnp.inf)

        row_max = lax.fori_loop(
            0,
            slots,
            lambda j, best: jnp.maximum(best, jnp.max(score(j), axis=1, keepdims=True)),
            jnp.full((tokens, 1), -jnp.inf, jnp.float32),
        )

        def add(slot, carry):
            total, summed = carry
            weights = jnp.exp2((score(slot) - row_max) * EXP2_SCALE)
            total += jnp.sum(weights, axis=1, keepdims=True)
            weights = weights.astype(jnp.bfloat16)
            return total, summed + jnp.dot(weights, part(value, slot), preferred_element_type=jnp.float32)

        zeros = jnp.zeros((tokens, 1), jnp.float32), jnp.zeros((tokens, HD), jnp.float32)
        total, summed = lax.fori_loop(0, slots, add, zeros)
        out[:, columns] = jnp.where(here.kept(), summed / total, 0.0).astype(out.dtype)
        return carry

    lax.fori_loop(0, query.shape[1] // HD, one_head, 0)


def attend_kernel(sizes, where, resident, placement, lengths, query_all, *refs):
    prompt_count, chips, ring, tokens = sizes
    here = Place(sizes, placement, lengths)
    arrays, refs = refs[:-9], refs[-9:]
    out_all, query_held, out_held, held_key, held_value, ones, bias, sems, fetch_sem = refs
    width = held_key.shape[1]
    kv_heads = width // HD
    span = query_all.shape[1] // kv_heads
    group = span // HD
    masked = bias.shape[1]

    def heads_of(kv_head):
        return pl.ds(pl.multiple_of(kv_head * span, span), span)

    def query_copy(kv_head):
        columns = heads_of(kv_head)
        return pltpu.make_async_copy(query_all.at[:, columns], query_held.at[:, columns], sems.at[0, kv_head])

    def out_copy(kv_head):
        columns = heads_of(kv_head)
        return pltpu.make_async_copy(out_held.at[:, columns], out_all.at[:, columns], sems.at[1, kv_head])

    for kv_head in range(kv_heads):
        query_copy(kv_head).start()

    def take(slot, carry):
        wanted = here.source(slot)
        for hop in range(ring):
            rows = pl.ds(pl.multiple_of((slot * ring + ring - 1 - hop) * tokens, tokens), tokens)
            seen = (ring - 1 - hop) * tokens >= here.first_key(slot)
            count = jnp.where(seen, 1.0, 0.0)
            ones[rows] = jnp.full((tokens, HD), count, jnp.float32).astype(ones.dtype)
            for kind, held in enumerate((held_key, held_value)):

                @pl.when(jnp.logical_not(seen))
                def _():
                    held[rows] = jnp.zeros((tokens, width), held.dtype)

                for source in range(here.blocks):
                    array, column = where[kind, source, hop]

                    @pl.when(seen & (wanted == source))
                    def _():
                        piece = arrays[array].at[:, column : column + width]
                        if resident:
                            held[rows] = piece[...]
                        else:
                            copy = pltpu.make_async_copy(piece, held.at[rows], fetch_sem)
                            copy.start()
                            copy.wait()

        return carry

    lax.fori_loop(0, here.slots, take, 0)
    own = lax.broadcasted_iota(jnp.int32, (tokens, masked), 0)
    key_row = lax.broadcasted_iota(jnp.int32, (tokens, masked), 1) - (masked - tokens)
    bias[...] = jnp.where(key_row <= own, 0.0, -jnp.inf)
    kept = here.kept()

    def of_head(kv_head):
        column = pl.ds(pl.multiple_of(kv_head * HD, HD), HD)
        columns = heads_of(kv_head)
        return query_held.at[:, columns], held_key.at[:, column], held_value.at[:, column], out_held.at[:, columns]

    def one_kv_head(kv_head, carry):
        least, most = carry
        query, key, value, out = of_head(kv_head)
        query_copy(kv_head).wait()
        keys, values = key[...], jnp.concatenate([value[...], ones[...]], axis=1)
        for tile in range(group // HEADS_PER_TILE):
            heads = range(tile * HEADS_PER_TILE, (tile + 1) * HEADS_PER_TILE)
            query_tile = jnp.concatenate([query[:, h * HD : (h + 1) * HD] for h in heads], axis=0)
            scores = matmul_nt(query_tile, keys) * EXP2_SCALE
            split = scores.shape[1] - masked
            tail = scores[:, split:].reshape(HEADS_PER_TILE, tokens, masked) + bias[...][None]
            tail = tail.reshape(HEADS_PER_TILE * tokens, masked)
            scores = tail if split == 0 else jnp.concatenate([scores[:, :split], tail], axis=1)
            weights = jnp.exp2(scores).astype(jnp.bfloat16)
            summed = jnp.dot(weights, values, preferred_element_type=jnp.float32)
            for i, h in enumerate(heads):
                part = summed[i * tokens : (i + 1) * tokens]
                total = part[:, HD:]
                least, most = jnp.minimum(least, total), jnp.maximum(most, total)
                out[:, h * HD : (h + 1) * HD] = jnp.where(kept, part[:, :HD] / total, 0.0).astype(out.dtype)
        out_copy(kv_head).start()
        return least, most

    zeros = jnp.zeros((tokens, HD), jnp.float32)
    least, most = lax.fori_loop(0, kv_heads, one_kv_head, (zeros + jnp.inf, zeros))
    safe = (jnp.min(least) > LEAST_TOTAL) & (jnp.max(most) < MOST_TOTAL)
    for kv_head in range(kv_heads):
        out_copy(kv_head).wait()

    @pl.when(jnp.logical_not(safe))
    def _():
        def again(kv_head, carry):
            query, key, value, out = of_head(kv_head)
            exact(here, query, key, value, out)
            out_copy(kv_head).start()
            out_copy(kv_head).wait()
            return carry

        lax.fori_loop(0, kv_heads, again, 0)


def attend(placement, lengths, query_rows, arrays, where, sizes, kv_heads):
    prompt_count, chips, ring, tokens = sizes
    slots = prompt_count + 1
    width = kv_heads * HD
    keys = slots * ring * tokens
    masked = tokens if tokens % HD == 0 else keys
    work = query_rows.size // HD * keys
    resident = sum(x.size * x.dtype.itemsize for x in arrays) <= RESIDENT_BYTES
    scalar, whole = pl.BlockSpec(memory_space=pltpu.SMEM), pl.BlockSpec(memory_space=pl.ANY)
    piece = pl.BlockSpec(memory_space=pltpu.VMEM) if resident else whole
    return pl.pallas_call(
        functools.partial(attend_kernel, sizes, where, resident),
        in_specs=[scalar, scalar, whole] + [piece] * len(arrays),
        out_specs=whole,
        scratch_shapes=[
            pltpu.VMEM(query_rows.shape, query_rows.dtype),
            pltpu.VMEM(query_rows.shape, query_rows.dtype),
            pltpu.VMEM((keys, width), jnp.bfloat16),
            pltpu.VMEM((keys, width), jnp.bfloat16),
            pltpu.VMEM((keys, HD), jnp.bfloat16),
            pltpu.VMEM((tokens, masked), jnp.float32),
            pltpu.SemaphoreType.DMA((2, kv_heads)),
            pltpu.SemaphoreType.DMA,
        ],
        out_shape=jax.ShapeDtypeStruct(query_rows.shape, query_rows.dtype),
        cost_estimate=pl.CostEstimate(flops=6 * work * HD, bytes_accessed=12 << 20, transcendentals=work),
        compiler_params=pltpu.CompilerParams(vmem_limit_bytes=2 * keys * width * 2 + (14 << 20)),
    )(placement, lengths, pltpu.with_memory_space_constraint(query_rows, pltpu.HBM), *arrays)


def after(x, *others):
    return lax.optimization_barrier((x, *others))[0]


def shards(query_rows, key_rows, value_rows, placement, lengths):
    blocks, ring = lax.axis_size("blk"), lax.axis_size("head")
    chips = blocks // CORES
    sizes = (blocks // 2, chips, ring, query_rows.shape[0])
    width = key_rows.shape[1]
    kv_heads = width // HD

    def next_hop(x):
        return lax.ppermute(x, "head", [(i, (i + 1) % ring) for i in range(ring)])

    def next_chip(x):
        return lax.ppermute(x, "blk", [(i, (i + CORES) % blocks) for i in range(blocks)])

    def other_core(x):
        return lax.ppermute(x, "blk", [(i, i ^ 1) for i in range(blocks)])

    columns, acrosses = [[key_rows], [value_rows]], [[], []]
    for hop in range(ring):
        for column, across in zip(columns, acrosses):
            x = after(column[hop], across[hop - 1]) if hop else column[hop]
            across.append(next_chip(x))
            if hop < ring - 1:
                column.append(next_hop(x))
    planes = [columns, acrosses]
    bundles = [[(0, c, hop) for c in range(2)] + [(1, c, hop - 1) for c in range(2) if hop] for hop in range(ring - 1)]
    bundles += [[(0, c, ring - 1), (1, c, ring - 2)] for c in range(2)] + [[(1, c, ring - 1)] for c in range(2)]
    for back in range(2, chips):
        planes.append([[next_chip(x) for x in part] for part in planes[-1]])
        bundles.append([(back, c, hop) for hop in range(ring) for c in range(2)])
    arrays, where = [], {}
    for back, plane in enumerate(planes):
        for c in range(2):
            for hop in range(ring):
                where[c, back * CORES, hop] = len(arrays), 0
                arrays.append(plane[c][hop])
    for bundle in bundles:
        for place, (back, c, hop) in enumerate(bundle):
            where[c, back * CORES + 1, hop] = len(arrays), place * width
        packed = jnp.concatenate([planes[back][c][hop] for back, c, hop in bundle], axis=1)
        for c in range(2):
            if bundle == bundles[ring - 1 + c]:
                packed = after(packed, planes[1][c][ring - 1])
        if bundle == bundles[ring + 2]:
            packed = after(packed, arrays[-1])
        arrays.append(other_core(packed))
    return attend(placement, lengths, query_rows, arrays, where, sizes, kv_heads)


def solution(mesh):
    rows = P(("grp", "blk", "head"), None)
    return jax.shard_map(
        shards,
        mesh=mesh,
        in_specs=(rows, rows, rows, P("grp"), P("grp")),
        out_specs=rows,
        check_vma=False,
    )
```

```python
import functools
import math

import jax
import jax.numpy as jnp
from jax import lax
from jax.experimental import pallas as pl
from jax.experimental.pallas import tpu as pltpu
from jax.sharding import PartitionSpec as P

HD = 128
CORES = 2
HEADS_PER_TILE = 2
EXP2_SCALE = math.log2(math.e) / math.sqrt(HD)
LEAST_TOTAL, MOST_TOTAL = 1e-20, 1e30


def matmul_nt(a, b):
    return lax.dot_general(a, b, (((1,), (1,)), ((), ())), preferred_element_type=jnp.float32)


class Place:
    def __init__(self, sizes, placement, lengths):
        self.prompt_count, self.chips, self.ring, self.tokens = sizes
        self.blocks, self.slots = self.chips * CORES, self.prompt_count + 1
        self.index, self.head = lax.axis_index("blk"), lax.axis_index("head")
        self.placement, self.lengths = placement, lengths
        self.block = placement[self.index]

    def source(self, slot):
        found = self.index
        for b in range(self.blocks):
            found = jnp.where(self.placement[b] == slot, b, found)
        found = jnp.where(slot == self.prompt_count, self.index, found)
        back = lax.shift_right_logical(self.index, 1) - lax.shift_right_logical(found, 1)
        return jnp.where(back < 0, back + self.chips, back) * CORES + ((self.index ^ found) & 1)

    def first_key(self, slot):
        own = (self.ring - 1 - self.head) * self.tokens
        return jnp.where(slot == self.prompt_count, own, jnp.where(self.block > slot, 0, self.ring * self.tokens))

    def kept(self):
        keep = jnp.int32(self.ring * self.tokens)
        for response in range(self.prompt_count):
            keep = jnp.where(self.block == self.prompt_count + response, self.lengths[response], keep)
        offsets = self.head * self.tokens + lax.broadcasted_iota(jnp.int32, (self.tokens, 1), 0)
        return offsets < keep


def exact(here, query, key, value, out):
    slots, tokens, rows = here.prompt_count + 1, here.tokens, here.ring * here.tokens
    key_row = lax.broadcasted_iota(jnp.int32, (tokens, rows), 1)
    newest_own = rows - tokens + lax.broadcasted_iota(jnp.int32, (tokens, rows), 0)

    def one_head(head, carry):
        columns = pl.ds(pl.multiple_of(head * HD, HD), HD)
        query_one = query[:, columns]

        def part(ref, slot):
            return ref[pl.ds(pl.multiple_of(slot * rows, rows), rows), :]

        def score(slot):
            newest = jnp.where(slot == here.prompt_count, newest_own, rows)
            seen = (key_row >= here.first_key(slot)) & (key_row <= newest)
            return jnp.where(seen, matmul_nt(query_one, part(key, slot)), -jnp.inf)

        row_max = lax.fori_loop(
            0,
            slots,
            lambda j, best: jnp.maximum(best, jnp.max(score(j), axis=1, keepdims=True)),
            jnp.full((tokens, 1), -jnp.inf, jnp.float32),
        )

        def add(slot, carry):
            total, summed = carry
            weights = jnp.exp2((score(slot) - row_max) * EXP2_SCALE)
            total += jnp.sum(weights, axis=1, keepdims=True)
            weights = weights.astype(jnp.bfloat16)
            return total, summed + jnp.dot(weights, part(value, slot), preferred_element_type=jnp.float32)

        zeros = jnp.zeros((tokens, 1), jnp.float32), jnp.zeros((tokens, HD), jnp.float32)
        total, summed = lax.fori_loop(0, slots, add, zeros)
        out[:, columns] = jnp.where(here.kept(), summed / total, 0.0).astype(out.dtype)
        return carry

    lax.fori_loop(0, query.shape[1] // HD, one_head, 0)


def fold_kernel(sizes, places, hops, counts, placement, lengths, query_all, *refs):
    prompt_count, chips, ring, tokens = sizes
    here = Place(sizes, placement, lengths)
    first, last = hops[0] == 0, hops[-1] == ring - 1
    refs = list(refs)
    arrays, state, stored = ([refs.pop(0) for _ in range(count)] for count in counts)
    out_all, held_key, held_value, ones, bias = refs[:5]
    width = held_key.shape[1]
    kv_heads = width // HD
    span = query_all.shape[1] // kv_heads
    group = span // HD
    masked = bias.shape[1]

    def heads_of(kv_head, size):
        return pl.ds(pl.multiple_of(kv_head * size, size), size)

    def take(slot, carry):
        wanted = here.source(slot)
        for i, hop in enumerate(reversed(hops)):
            rows = pl.ds(pl.multiple_of((slot * len(hops) + i) * tokens, tokens), tokens)
            seen = (ring - 1 - hop) * tokens >= here.first_key(slot)
            ones[rows] = jnp.full((tokens, HD), jnp.where(seen, 1.0, 0.0), jnp.float32).astype(ones.dtype)
            for kind, held in enumerate((held_key, held_value)):

                @pl.when(jnp.logical_not(seen))
                def _():
                    held[rows] = jnp.zeros((tokens, width), held.dtype)

                for source in range(here.blocks):
                    array, column = places[kind, source, hop]

                    @pl.when(seen & (wanted == source))
                    def _():
                        held[rows] = arrays[array][:, column : column + width]

        return carry

    lax.fori_loop(0, here.slots, take, 0)
    if first:
        own = lax.broadcasted_iota(jnp.int32, (tokens, masked), 0)
        key_row = lax.broadcasted_iota(jnp.int32, (tokens, masked), 1) - (masked - tokens)
        bias[...] = jnp.where(key_row <= own, 0.0, -jnp.inf)
    kept = here.kept()
    out = refs[5] if last else out_all

    def one_kv_head(kv_head, carry):
        least, most = carry
        query = query_all.at[:, heads_of(kv_head, span)]
        column = heads_of(kv_head, HD)
        keys, values = held_key[:, column], jnp.concatenate([held_value[:, column], ones[...]], axis=1)
        sums = heads_of(kv_head, 2 * span)
        for tile in range(group // HEADS_PER_TILE):
            these = range(tile * HEADS_PER_TILE, (tile + 1) * HEADS_PER_TILE)
            query_tile = jnp.concatenate([query[:, h * HD : (h + 1) * HD] for h in these], axis=0)
            scores = matmul_nt(query_tile, keys) * EXP2_SCALE
            if first:
                split = scores.shape[1] - masked
                tail = scores[:, split:].reshape(HEADS_PER_TILE, tokens, masked) + bias[...][None]
                tail = tail.reshape(HEADS_PER_TILE * tokens, masked)
                scores = tail if split == 0 else jnp.concatenate([scores[:, :split], tail], axis=1)
            weights = jnp.exp2(scores).astype(jnp.bfloat16)
            summed = jnp.dot(weights, values, preferred_element_type=jnp.float32)
            for i, h in enumerate(these):
                part = summed[i * tokens : (i + 1) * tokens]
                both = slice(h * 2 * HD, (h + 1) * 2 * HD)
                if not first:
                    part = part + state[0].at[:, sums][:, both]
                if last:
                    total = part[:, HD:]
                    least, most = jnp.minimum(least, total), jnp.maximum(most, total)
                    result = jnp.where(kept, part[:, :HD] / total, 0.0).astype(out.dtype)
                    out.at[:, heads_of(kv_head, span)][:, h * HD : (h + 1) * HD] = result
                else:
                    out.at[:, sums][:, both] = part
        if last:
            out_copy(kv_head).start()
        return least, most

    def out_copy(kv_head):
        columns = heads_of(kv_head, span)
        return pltpu.make_async_copy(out.at[:, columns], out_all.at[:, columns], refs[6].at[kv_head])

    zeros = jnp.zeros((tokens, HD), jnp.float32)
    least, most = lax.fori_loop(0, kv_heads, one_kv_head, (zeros + jnp.inf, zeros))
    if not last:
        return
    safe = (jnp.min(least) > LEAST_TOTAL) & (jnp.max(most) < MOST_TOTAL)
    for kv_head in range(kv_heads):
        out_copy(kv_head).wait()

    @pl.when(jnp.logical_not(safe))
    def _():
        all_key, all_value, sem = refs[7:]

        def fetch(slot, carry):
            wanted = here.source(slot)
            for source in range(here.blocks):

                @pl.when(wanted == source)
                def _():
                    for back in range(ring):
                        first = (slot * ring + ring - 1 - back) * tokens
                        rows = pl.ds(pl.multiple_of(first, tokens), tokens)
                        for kind, held in enumerate((all_key, all_value)):
                            array, column = places[kind, source, back, None]
                            piece = stored[array].at[:, column : column + width]
                            copy = pltpu.make_async_copy(piece, held.at[rows], sem)
                            copy.start()
                            copy.wait()

            return carry

        lax.fori_loop(0, here.slots, fetch, 0)

        def again(kv_head, carry):
            columns, column = heads_of(kv_head, span), heads_of(kv_head, HD)
            exact(here, query_all.at[:, columns], all_key.at[:, column], all_value.at[:, column], out.at[:, columns])
            out_copy(kv_head).start()
            out_copy(kv_head).wait()
            return carry

        lax.fori_loop(0, kv_heads, again, 0)


def fold(placement, lengths, query_rows, arrays, where, sizes, hops, state):
    prompt_count, chips, ring, tokens = sizes
    slots = prompt_count + 1
    last = hops[-1] == ring - 1
    wanted = [(kind, source, hop) for kind in range(2) for source in range(chips * CORES) for hop in hops]
    used = sorted({where[piece][0] for piece in wanted})
    places = {piece: (used.index(where[piece][0]), where[piece][1]) for piece in wanted}
    width = arrays[0].shape[1]
    kv_heads = width // HD
    keys = slots * len(hops) * tokens
    masked = tokens if tokens % HD == 0 else keys
    scalar, whole, near = (pl.BlockSpec(memory_space=x) for x in (pltpu.SMEM, pl.ANY, pltpu.VMEM))
    operands = [arrays[a] for a in used]
    if state is not None:
        operands.append(state)
    scratch = [
        pltpu.VMEM((keys, width), jnp.bfloat16),
        pltpu.VMEM((keys, width), jnp.bfloat16),
        pltpu.VMEM((keys, HD), jnp.bfloat16),
        pltpu.VMEM((tokens, masked), jnp.float32),
    ]
    specs = [scalar, scalar, near] + [near] * len(operands)
    stored = []
    if last:
        stored = arrays
        places |= {(*piece, None): at for piece, at in where.items()}
        scratch += [
            pltpu.VMEM(query_rows.shape, query_rows.dtype),
            pltpu.SemaphoreType.DMA((kv_heads,)),
            pltpu.VMEM((slots * ring * tokens, width), jnp.bfloat16),
            pltpu.VMEM((slots * ring * tokens, width), jnp.bfloat16),
            pltpu.SemaphoreType.DMA,
        ]
        out_shape, out_spec, aliases = query_rows.shape, whole, {}
    else:
        out_shape, out_spec = (tokens, 2 * query_rows.shape[1]), near
        aliases = {} if state is None else {3 + len(used): 0}
    counts = len(used), int(state is not None), len(stored)
    work = tokens * keys * query_rows.shape[1] // HD
    scoped = 2 * (keys + (slots * ring * tokens if last else 0)) * width * 2 + (12 << 20)
    return pl.pallas_call(
        functools.partial(fold_kernel, sizes, places, hops, counts),
        in_specs=specs + [whole] * len(stored),
        out_specs=out_spec,
        scratch_shapes=scratch,
        out_shape=jax.ShapeDtypeStruct(out_shape, query_rows.dtype if last else jnp.float32),
        input_output_aliases=aliases,
        cost_estimate=pl.CostEstimate(flops=6 * work * HD, bytes_accessed=4 << 20, transcendentals=work),
        compiler_params=pltpu.CompilerParams(vmem_limit_bytes=scoped),
    )(placement, lengths, query_rows, *operands, *stored)


def after(x, *others):
    return lax.optimization_barrier((x, *others))[0]


def shards(query_rows, key_rows, value_rows, placement, lengths):
    blocks, ring = lax.axis_size("blk"), lax.axis_size("head")
    chips = blocks // CORES
    sizes = (blocks // 2, chips, ring, query_rows.shape[0])
    width = key_rows.shape[1]
    kv_heads = width // HD

    def next_hop(x):
        return lax.ppermute(x, "head", [(i, (i + 1) % ring) for i in range(ring)])

    def next_chip(x):
        return lax.ppermute(x, "blk", [(i, (i + CORES) % blocks) for i in range(blocks)])

    def other_core(x):
        return lax.ppermute(x, "blk", [(i, i ^ 1) for i in range(blocks)])

    planes = [[[key_rows], [value_rows]]] + [[[], []] for _ in range(chips - 1)]
    arrays, where = [], {}

    def bundle(*items):
        for place, (back, c, hop) in enumerate(items):
            where[c, back * CORES + 1, hop] = len(arrays), place * width
        packed = jnp.concatenate([planes[back][c][hop] for back, c, hop in items], axis=1)
        arrays.append(other_core(after(packed, state) if items[0][2] == ring - 1 and items[0][0] else packed))

    cut, state = ring // 2, None

    for hop in range(ring):
        if hop == ring - 1:
            state = fold(placement, lengths, query_rows, arrays, where, sizes, tuple(range(cut)), None)
        for column, across in zip(planes[0], planes[1]):
            x = after(column[hop], across[hop - 1]) if hop else column[hop]
            across.append(next_chip(x))
            if hop < ring - 1:
                column.append(next_hop(x))
        for back in range(2, chips):
            for c in range(2):
                planes[back][c].append(next_chip(planes[back - 1][c][hop]))
        for back, plane in enumerate(planes):
            for c in range(2):
                where[c, back * CORES, hop] = len(arrays), 0
                arrays.append(plane[c][hop])
        everything = [(back, c, hop) for back in range(chips) for c in range(2)]
        if hop < cut:
            for piece in everything:
                bundle(piece)
        elif hop < ring - 1:
            bundle(*everything)
        else:
            bundle(*everything[:2])
            bundle(*everything[2:])
    return fold(placement, lengths, query_rows, arrays, where, sizes, tuple(range(cut, ring)), state)


def solution(mesh):
    rows = P(("grp", "blk", "head"), None)
    return jax.shard_map(
        shards,
        mesh=mesh,
        in_specs=(rows, rows, rows, P("grp"), P("grp")),
        out_specs=rows,
        check_vma=False,
    )
```

```python
import functools
import math

import jax
import jax.numpy as jnp
from jax import lax
from jax.experimental import pallas as pl
from jax.experimental.pallas import tpu as pltpu
from jax.sharding import PartitionSpec as P

HD = 128
CORES = 2
HEADS_PER_TILE = 4
RESIDENT_BYTES = 16 << 20
EXP2_SCALE = math.log2(math.e) / math.sqrt(HD)
LEAST_TOTAL, MOST_TOTAL = 1e-20, 1e30


def matmul_nt(a, b):
    return lax.dot_general(a, b, (((1,), (1,)), ((), ())), preferred_element_type=jnp.float32)


class Place:
    def __init__(self, sizes, placement, lengths):
        self.prompt_count, self.chips, self.ring, self.tokens = sizes
        self.blocks, self.slots = self.chips * CORES, self.prompt_count + 1
        self.index, self.head = lax.axis_index("blk"), lax.axis_index("head")
        self.placement, self.lengths = placement, lengths
        self.block = placement[self.index]

    def source(self, slot):
        found = self.index
        for b in range(self.blocks):
            found = jnp.where(self.placement[b] == slot, b, found)
        found = jnp.where(slot == self.prompt_count, self.index, found)
        back = lax.shift_right_logical(self.index, 1) - lax.shift_right_logical(found, 1)
        return jnp.where(back < 0, back + self.chips, back) * CORES + ((self.index ^ found) & 1)

    def first_key(self, slot):
        own = (self.ring - 1 - self.head) * self.tokens
        return jnp.where(slot == self.prompt_count, own, jnp.where(self.block > slot, 0, self.ring * self.tokens))

    def kept(self):
        keep = jnp.int32(self.ring * self.tokens)
        for response in range(self.prompt_count):
            keep = jnp.where(self.block == self.prompt_count + response, self.lengths[response], keep)
        offsets = self.head * self.tokens + lax.broadcasted_iota(jnp.int32, (self.tokens, 1), 0)
        return offsets < keep


def exact(here, query, key, value, out):
    slots, tokens, rows = here.prompt_count + 1, here.tokens, here.ring * here.tokens
    key_row = lax.broadcasted_iota(jnp.int32, (tokens, rows), 1)
    newest_own = rows - tokens + lax.broadcasted_iota(jnp.int32, (tokens, rows), 0)

    def one_head(head, carry):
        columns = pl.ds(pl.multiple_of(head * HD, HD), HD)
        query_one = query[:, columns]

        def part(ref, slot):
            return ref[pl.ds(pl.multiple_of(slot * rows, rows), rows), :]

        def score(slot):
            newest = jnp.where(slot == here.prompt_count, newest_own, rows)
            seen = (key_row >= here.first_key(slot)) & (key_row <= newest)
            return jnp.where(seen, matmul_nt(query_one, part(key, slot)), -jnp.inf)

        row_max = lax.fori_loop(
            0,
            slots,
            lambda j, best: jnp.maximum(best, jnp.max(score(j), axis=1, keepdims=True)),
            jnp.full((tokens, 1), -jnp.inf, jnp.float32),
        )

        def add(slot, carry):
            total, summed = carry
            weights = jnp.exp2((score(slot) - row_max) * EXP2_SCALE)
            total += jnp.sum(weights, axis=1, keepdims=True)
            weights = weights.astype(jnp.bfloat16)
            return total, summed + jnp.dot(weights, part(value, slot), preferred_element_type=jnp.float32)

        zeros = jnp.zeros((tokens, 1), jnp.float32), jnp.zeros((tokens, HD), jnp.float32)
        total, summed = lax.fori_loop(0, slots, add, zeros)
        out[:, columns] = jnp.where(here.kept(), summed / total, 0.0).astype(out.dtype)
        return carry

    lax.fori_loop(0, query.shape[1] // HD, one_head, 0)


def attend_kernel(sizes, where, resident, placement, lengths, query_all, *refs):
    prompt_count, chips, ring, tokens = sizes
    here = Place(sizes, placement, lengths)
    arrays, refs = refs[:-9], refs[-9:]
    out_all, query_held, out_held, held_key, held_value, ones, bias, sems, fetch_sem = refs
    width = held_key.shape[1]
    kv_heads = width // HD
    span = query_all.shape[1] // kv_heads
    group = span // HD
    masked = bias.shape[1]

    def heads_of(kv_head):
        return pl.ds(pl.multiple_of(kv_head * span, span), span)

    def query_copy(kv_head):
        columns = heads_of(kv_head)
        return pltpu.make_async_copy(query_all.at[:, columns], query_held.at[:, columns], sems.at[0, kv_head])

    def out_copy(kv_head):
        columns = heads_of(kv_head)
        return pltpu.make_async_copy(out_held.at[:, columns], out_all.at[:, columns], sems.at[1, kv_head])

    for kv_head in range(kv_heads):
        query_copy(kv_head).start()

    def take(slot, carry):
        wanted = here.source(slot)
        for hop in range(ring):
            rows = pl.ds(pl.multiple_of((slot * ring + ring - 1 - hop) * tokens, tokens), tokens)
            seen = (ring - 1 - hop) * tokens >= here.first_key(slot)
            count = jnp.where(seen, 1.0, 0.0)
            ones[rows] = jnp.full((tokens, HD), count, jnp.float32).astype(ones.dtype)
            for kind, held in enumerate((held_key, held_value)):

                @pl.when(jnp.logical_not(seen))
                def _():
                    held[rows] = jnp.zeros((tokens, width), held.dtype)

                for source in range(here.blocks):
                    array, column = where[kind, source, hop]

                    @pl.when(seen & (wanted == source))
                    def _():
                        piece = arrays[array].at[:, column : column + width]
                        if resident:
                            held[rows] = piece[...]
                        else:
                            copy = pltpu.make_async_copy(piece, held.at[rows], fetch_sem)
                            copy.start()
                            copy.wait()

        return carry

    lax.fori_loop(0, here.slots, take, 0)
    own = lax.broadcasted_iota(jnp.int32, (tokens, masked), 0)
    key_row = lax.broadcasted_iota(jnp.int32, (tokens, masked), 1) - (masked - tokens)
    bias[...] = jnp.where(key_row <= own, 0.0, -jnp.inf)
    kept = here.kept()

    def of_head(kv_head):
        column = pl.ds(pl.multiple_of(kv_head * HD, HD), HD)
        columns = heads_of(kv_head)
        return query_held.at[:, columns], held_key.at[:, column], held_value.at[:, column], out_held.at[:, columns]

    def one_kv_head(kv_head, carry):
        least, most = carry
        query, key, value, out = of_head(kv_head)
        query_copy(kv_head).wait()
        keys, values = key[...], jnp.concatenate([value[...], ones[...]], axis=1)
        for tile in range(group // HEADS_PER_TILE):
            heads = range(tile * HEADS_PER_TILE, (tile + 1) * HEADS_PER_TILE)
            query_tile = jnp.concatenate([query[:, h * HD : (h + 1) * HD] for h in heads], axis=0)
            scores = matmul_nt(query_tile, keys) * EXP2_SCALE
            split = scores.shape[1] - masked
            tail = scores[:, split:].reshape(HEADS_PER_TILE, tokens, masked) + bias[...][None]
            tail = tail.reshape(HEADS_PER_TILE * tokens, masked)
            scores = tail if split == 0 else jnp.concatenate([scores[:, :split], tail], axis=1)
            weights = jnp.exp2(scores).astype(jnp.bfloat16)
            summed = jnp.dot(weights, values, preferred_element_type=jnp.float32)
            for i, h in enumerate(heads):
                part = summed[i * tokens : (i + 1) * tokens]
                total = part[:, HD:]
                least, most = jnp.minimum(least, total), jnp.maximum(most, total)
                out[:, h * HD : (h + 1) * HD] = jnp.where(kept, part[:, :HD] / total, 0.0).astype(out.dtype)
        out_copy(kv_head).start()
        return least, most

    zeros = jnp.zeros((tokens, HD), jnp.float32)
    least, most = lax.fori_loop(0, kv_heads, one_kv_head, (zeros + jnp.inf, zeros))
    safe = (jnp.min(least) > LEAST_TOTAL) & (jnp.max(most) < MOST_TOTAL)
    for kv_head in range(kv_heads):
        out_copy(kv_head).wait()

    @pl.when(jnp.logical_not(safe))
    def _():
        def again(kv_head, carry):
            query, key, value, out = of_head(kv_head)
            exact(here, query, key, value, out)
            out_copy(kv_head).start()
            out_copy(kv_head).wait()
            return carry

        lax.fori_loop(0, kv_heads, again, 0)


def attend(placement, lengths, query_rows, arrays, where, sizes, kv_heads):
    prompt_count, chips, ring, tokens = sizes
    slots = prompt_count + 1
    width = kv_heads * HD
    keys = slots * ring * tokens
    masked = tokens if tokens % HD == 0 else keys
    work = query_rows.size // HD * keys
    resident = sum(x.size * x.dtype.itemsize for x in arrays) <= RESIDENT_BYTES
    scalar, whole = pl.BlockSpec(memory_space=pltpu.SMEM), pl.BlockSpec(memory_space=pl.ANY)
    piece = pl.BlockSpec(memory_space=pltpu.VMEM) if resident else whole
    return pl.pallas_call(
        functools.partial(attend_kernel, sizes, where, resident),
        in_specs=[scalar, scalar, whole] + [piece] * len(arrays),
        out_specs=whole,
        scratch_shapes=[
            pltpu.VMEM(query_rows.shape, query_rows.dtype),
            pltpu.VMEM(query_rows.shape, query_rows.dtype),
            pltpu.VMEM((keys, width), jnp.bfloat16),
            pltpu.VMEM((keys, width), jnp.bfloat16),
            pltpu.VMEM((keys, HD), jnp.bfloat16),
            pltpu.VMEM((tokens, masked), jnp.float32),
            pltpu.SemaphoreType.DMA((2, kv_heads)),
            pltpu.SemaphoreType.DMA,
        ],
        out_shape=jax.ShapeDtypeStruct(query_rows.shape, query_rows.dtype),
        cost_estimate=pl.CostEstimate(flops=6 * work * HD, bytes_accessed=12 << 20, transcendentals=work),
        compiler_params=pltpu.CompilerParams(vmem_limit_bytes=2 * keys * width * 2 + (20 << 20)),
    )(placement, lengths, pltpu.with_memory_space_constraint(query_rows, pltpu.HBM), *arrays)


def after(x, *others):
    return lax.optimization_barrier((x, *others))[0]


def shards(query_rows, key_rows, value_rows, placement, lengths):
    blocks, ring = lax.axis_size("blk"), lax.axis_size("head")
    chips = blocks // CORES
    sizes = (blocks // 2, chips, ring, query_rows.shape[0])
    width = key_rows.shape[1]
    kv_heads = width // HD

    def next_hop(x):
        return lax.ppermute(x, "head", [(i, (i + 1) % ring) for i in range(ring)])

    def next_chip(x):
        return lax.ppermute(x, "blk", [(i, (i + CORES) % blocks) for i in range(blocks)])

    def other_core(x):
        return lax.ppermute(x, "blk", [(i, i ^ 1) for i in range(blocks)])

    columns, acrosses = [[key_rows], [value_rows]], [[], []]
    for hop in range(ring):
        for column, across in zip(columns, acrosses):
            x = after(column[hop], across[hop - 1]) if hop else column[hop]
            across.append(next_chip(x))
            if hop < ring - 1:
                column.append(next_hop(x))
    planes = [columns, acrosses]
    bundles = [[(0, c, hop) for c in range(2)] + [(1, c, hop - 1) for c in range(2) if hop] for hop in range(ring - 1)]
    bundles += [[(0, c, ring - 1), (1, c, ring - 2)] for c in range(2)] + [[(1, c, ring - 1)] for c in range(2)]
    for back in range(2, chips):
        planes.append([[next_chip(x) for x in part] for part in planes[-1]])
        bundles.append([(back, c, hop) for hop in range(ring) for c in range(2)])
    arrays, where = [], {}
    for back, plane in enumerate(planes):
        for c in range(2):
            for hop in range(ring):
                where[c, back * CORES, hop] = len(arrays), 0
                arrays.append(plane[c][hop])
    for bundle in bundles:
        for place, (back, c, hop) in enumerate(bundle):
            where[c, back * CORES + 1, hop] = len(arrays), place * width
        packed = jnp.concatenate([planes[back][c][hop] for back, c, hop in bundle], axis=1)
        for c in range(2):
            if bundle == bundles[ring - 1 + c]:
                packed = after(packed, planes[1][c][ring - 1])
        if bundle == bundles[ring + 2]:
            packed = after(packed, arrays[-1])
        arrays.append(other_core(packed))
    return attend(placement, lengths, query_rows, arrays, where, sizes, kv_heads)


def solution(mesh):
    rows = P(("grp", "blk", "head"), None)
    return jax.shard_map(
        shards,
        mesh=mesh,
        in_specs=(rows, rows, rows, P("grp"), P("grp")),
        out_specs=rows,
        check_vma=False,
    )
```
